32 devices in a mesh: dp: 4 (over y, x), ctx: 4 (over z), tensor: 2 (over core).
Axes of the slice: x: 2, y: 2, z: 4, core: 2. Of those that a mesh axis runs over, the one named last changes fastest.
Arguments:
- seq_in: bfloat16 [4, 2048, 5120], P('dp', 'ctx', 'tensor'), may hold values from -6 to 6
- gate_in: bfloat16 [4, 2048, 5120], P('dp', 'ctx', 'tensor'), may hold values from -96 to 96
- keys_in: bfloat16 [4, 2048, 128], P('dp', 'ctx'), may hold values from -0.5 to 0.5
- queries_in: bfloat16 [4, 2048, 128], P('dp', 'ctx'), may hold values from -0.5 to 0.5
- step_rate: float32 [4, 2048, 80], P('dp', 'ctx', 'tensor'), may hold values from 0 to 1, as said below
- doc_starts: int32 [4, 4], P('dp', 'ctx'), may hold values from 0 to 512, as said below
- skip_gain: float32 [80], P('tensor'), may hold values from 0.5 to 1.5
- norm_gain: float32 [5120], P('tensor'), may hold values from 0.5 to 1.5
- prompt_in: bfloat16 [32, 5120], P(None, 'tensor'), may hold values from -6 to 6
- prompt_keys: bfloat16 [32, 128], replicated, may hold values from -0.5 to 0.5
- prompt_rate: float32 [32, 80], P(None, 'tensor'), may hold values from 0.01 to 0.1
- start_state: float32 [128, 5120], P(None, 'tensor'), may hold values from -6 to 6
- out_grad: bfloat16 [4, 2048, 5120], P('dp', 'ctx', 'tensor'), may hold values from -6 to 6
Outputs:
- normed: bfloat16 [4, 2048, 5120], P('dp', 'ctx', 'tensor')
- grad_in: bfloat16 [4, 2048, 5120], P('dp', 'ctx', 'tensor')
- grad_gate: bfloat16 [4, 2048, 5120], P('dp', 'ctx', 'tensor')
- grad_prompt: float32 [32, 5120], P(None, 'tensor')
- grad_start: float32 [128, 5120], P(None, 'tensor')
The draws below stay inside these ranges and needn't reach their ends.
Inputs may be any that keep to these rules, and one draw needn't show every extreme that they name: doc_starts[b, c] is the position within block c of sequence b at which a new document begins, 512 where none begins in that block; at most one begins in a block. `step_rate`: Positive.
All inputs are finite; a program needn't handle non-finite values.
Results may differ from the reference program's by a relative error of at most 0.006.
Values sent between devices are 32-bit elements; how exact they have to be, the bound alone decides.
No kernel may reach another device: no remote copies, remote signals or barrier semaphores. Data moves between devices by JAX's collectives and lax.ppermute only.
A program may use at most 256 MiB of HBM per device.

```python
import math
import jax
import jax.numpy as jnp
from jax import lax

INNER = 5120
STATE = 128
HEAD_DIM = 64
HEAD_TOTAL = 80
TOK_DEV = 512
PROMPT = 32
BATCH_SEQUENCES = 4
SEQUENCE_LENGTH = 2048


def log_spread(key, shape, lowest, highest):
    return jnp.exp(jax.random.uniform(key, shape, jnp.float32, jnp.log(lowest), jnp.log(highest)))


def draw_step_rate(key, part):
    key = jax.random.fold_in(key, 11)
    key_entries = jax.random.split(key, 7)
    slow_share = 0.5
    blocks_per = SEQUENCE_LENGTH // TOK_DEV
    choose = jax.random.uniform(key_entries[0], (BATCH_SEQUENCES, 1, HEAD_TOTAL))
    slow_rate = log_spread(key_entries[1], (BATCH_SEQUENCES, 1, HEAD_TOTAL), 0.05 / SEQUENCE_LENGTH, 0.5 / SEQUENCE_LENGTH)
    fast_rate = log_spread(key_entries[2], (BATCH_SEQUENCES, 1, HEAD_TOTAL), 4.0 / TOK_DEV, 8.0 / TOK_DEV)
    baseline_rate = jnp.where(choose < slow_share, slow_rate, fast_rate)
    each_block_count = log_spread(key_entries[3], (BATCH_SEQUENCES, blocks_per, 1, HEAD_TOTAL), 0.5, 2.0)
    each_block_count = jnp.broadcast_to(each_block_count, (BATCH_SEQUENCES, blocks_per, TOK_DEV, HEAD_TOTAL)).reshape(BATCH_SEQUENCES, SEQUENCE_LENGTH, HEAD_TOTAL)
    jaggedness = log_spread(key_entries[4], (BATCH_SEQUENCES, SEQUENCE_LENGTH, HEAD_TOTAL), 0.5, 2.0)
    cluster_mask = jax.random.uniform(key_entries[5], (BATCH_SEQUENCES, SEQUENCE_LENGTH, 1)) < 3.0 / SEQUENCE_LENGTH
    cluster_length = jax.random.uniform(key_entries[6], (BATCH_SEQUENCES, SEQUENCE_LENGTH, HEAD_TOTAL), jnp.float32, 0.2, 0.7)
    return (baseline_rate * each_block_count * jaggedness + jnp.where(cluster_mask, cluster_length, 0.0)).astype(jnp.float32)


def draw_doc_starts(key, part):
    key = jax.random.fold_in(key, 23)
    key_entries = jax.random.split(key, 2)
    where_at = jax.random.randint(key_entries[0], (BATCH_SEQUENCES, SEQUENCE_LENGTH // TOK_DEV), 0, TOK_DEV)
    roll = jax.random.randint(key_entries[1], (BATCH_SEQUENCES, SEQUENCE_LENGTH // TOK_DEV), 0, 4)
    return jnp.where(roll == 0, where_at, TOK_DEV).astype(jnp.int32)


def draw_gate_in(key, part):
    key = jax.random.fold_in(key, 37)
    key_entries = jax.random.split(key, 3)
    row_scale = log_spread(key_entries[0], (BATCH_SEQUENCES, SEQUENCE_LENGTH, 1), 0.3, 3.0)
    ramp = 1.0 + 0.8 * jnp.arange(INNER, dtype=jnp.float32) / INNER
    col_scale = log_spread(key_entries[1], (1, 1, INNER), 0.3, 3.0) * ramp
    base_value = jnp.clip(jax.random.normal(key_entries[2], (BATCH_SEQUENCES, SEQUENCE_LENGTH, INNER), jnp.float32), -5.0, 5.0)
    return (base_value * row_scale * col_scale).astype(jnp.bfloat16)


def shard_levels(own_key, shape, cuts, low, top_value):
    def one(position, blocks):
        heights = jax.random.uniform(jax.random.fold_in(jax.random.fold_in(own_key, 6), position), (blocks,), jnp.float32, low / len(cuts), top_value / len(cuts))
        return jnp.repeat(jnp.exp(heights), shape[position] // blocks).reshape((-1,) + (1,) * (len(shape) - position - 1))

    factor_of = one(*cuts[0])
    for cut in cuts[1:]:
        factor_of = factor_of * one(*cut)
    return factor_of


def normal_values(own_key, extent, scale, bound, cuts=(), held_as=jnp.bfloat16):
    factor_of = shard_levels(own_key, extent, cuts, -0.22, 0.18) if cuts else 1.0
    drawn = jax.random.normal(own_key, extent, jnp.float32) * scale * factor_of
    return jnp.minimum(jnp.maximum(drawn, -bound), bound).astype(held_as)


def setup_inputs(seed: int = 0) -> dict:
    key_of = jax.random.split(jax.random.key(seed), 14)
    return {
        "seq_in": normal_values(key_of[0], (BATCH_SEQUENCES, SEQUENCE_LENGTH, INNER), 1.0, 6.0, ((0, 4), (1, 4), (2, 2))),
        "gate_in": draw_gate_in(jax.random.fold_in(key_of[13], 71), 0),
        "keys_in": normal_values(key_of[2], (BATCH_SEQUENCES, SEQUENCE_LENGTH, STATE), 0.09, 0.5, ((0, 4), (1, 4))),
        "queries_in": normal_values(key_of[3], (BATCH_SEQUENCES, SEQUENCE_LENGTH, STATE), 0.09, 0.5, ((0, 4), (1, 4))),
        "step_rate": draw_step_rate(jax.random.fold_in(key_of[13], 71), 0),
        "doc_starts": draw_doc_starts(jax.random.fold_in(key_of[13], 71), 0),
        "skip_gain": jnp.clip(0.5 + 1.0 * jax.random.uniform(key_of[6], (HEAD_TOTAL,), jnp.float32) ** shard_levels(key_of[6], (HEAD_TOTAL,), ((0, 2),), -0.2, 0.2), 0.5, 1.5),
        "norm_gain": jnp.clip(1.0 + 0.1 * jax.random.normal(key_of[7], (INNER,), jnp.float32), 0.5, 1.5),
        "prompt_in": normal_values(key_of[8], (PROMPT, INNER), 1.0, 6.0, ((1, 2),)),
        "prompt_keys": normal_values(key_of[9], (PROMPT, STATE), 0.09, 0.5),
        "prompt_rate": jnp.clip(jnp.exp(math.log(0.1) - 2.3025851 * jax.random.uniform(key_of[10], (PROMPT, HEAD_TOTAL), jnp.float32) ** shard_levels(key_of[10], (PROMPT, HEAD_TOTAL), ((1, 2),), -0.2, 0.2)), 0.01, 0.1),
        "start_state": normal_values(key_of[11], (STATE, INNER), 1.0, 6.0, ((1, 2),), jnp.float32),
        "out_grad": normal_values(key_of[12], (BATCH_SEQUENCES, SEQUENCE_LENGTH, INNER), 1.0, 6.0, ((0, 4), (1, 4), (2, 2))),
    }


EPSILON = 1e-05

def expand(per_head):
    return jnp.repeat(per_head, HEAD_DIM, axis=-1)

def silu_parts(gate_value):
    sigmoid_gate = jax.nn.sigmoid(gate_value)
    return (gate_value * sigmoid_gate, sigmoid_gate * (1.0 + gate_value * (1.0 - sigmoid_gate)))

def prompt_state(prompt_in, prompt_keys, prompt_rate, start_state):
    suffix_rate = jnp.cumsum(prompt_rate[::-1], axis=0)[::-1] - prompt_rate
    weight_cols = expand(jnp.exp(-suffix_rate))
    carry_cols = expand(jnp.exp(-lax.optimization_barrier(jnp.sum(prompt_rate, axis=0))))
    spread = weight_cols * prompt_in.astype(jnp.float32)
    prompt_field = jnp.dot(prompt_keys.astype(jnp.float32).T, spread, precision=lax.Precision.HIGHEST)
    return (prompt_field + carry_cols * start_state, weight_cols, carry_cols)

def derive(start_grad, prompt_keys, weight_cols, carry_cols):
    prompt_grad = weight_cols * jnp.dot(prompt_keys.astype(jnp.float32), start_grad, precision=lax.Precision.HIGHEST)
    return (prompt_grad, carry_cols * start_grad)

def tables(step_block, doc_start):
    block_rows = step_block.shape[0]
    positions = jnp.arange(block_rows, dtype=jnp.int32)
    cumulative = jnp.cumsum(step_block, axis=0)
    before = cumulative - step_block
    cum_end = cumulative[block_rows - 1]
    has_start = doc_start < block_rows
    ex_start = lax.optimization_barrier(jnp.sum(jnp.where((positions == doc_start)[:, None], before, 0.0), axis=0))
    after = (positions >= doc_start)[:, None]
    weight_in = jnp.where(after, 0.0, jnp.exp(-cumulative))
    weight_start = jnp.where(after, jnp.exp(-jnp.where(after, cumulative - ex_start, 0.0)), 0.0)
    tail = (positions >= jnp.where(has_start, doc_start, 0))[:, None]
    weight_out = jnp.where(tail, jnp.exp(-(cum_end - cumulative)), 0.0)
    through = jnp.where(has_start, 0.0, jnp.exp(-cum_end))
    exit_start = jnp.where(has_start, jnp.exp(-(cum_end - ex_start)), 0.0)
    return (cumulative, weight_in, weight_start, weight_out, through, exit_start)

def make_mixing(key_block, query_block, cumulative, doc_start):
    block_rows = cumulative.shape[0]
    positions = jnp.arange(block_rows, dtype=jnp.int32)
    after = positions >= doc_start
    same_doc = (positions[None, :] <= positions[:, None]) & (after[:, None] == after[None, :])
    scores = jnp.dot(query_block, key_block.T, preferred_element_type=jnp.float32)
    cum_heads = cumulative.T
    log_gap = cum_heads[:, :, None] - cum_heads[:, None, :]
    decays = jnp.where(same_doc[None], jnp.exp(-jnp.where(same_doc[None], log_gap, 0.0)), 0.0)
    return (scores[None] * decays).astype(jnp.bfloat16)

def weigh(weights, row_block):
    return (weights.T[:, :, None] * row_block.astype(jnp.float32)[None]).astype(jnp.bfloat16)

def reference(seq_in, gate_in, keys_in, queries_in, step_rate, doc_starts, skip_gain, norm_gain, prompt_in, prompt_keys, prompt_rate, start_state, out_grad):
    start_field, weight_cols, carry_cols = prompt_state(prompt_in, prompt_keys, prompt_rate, start_state)
    start_low = start_field.astype(jnp.bfloat16)
    skip_cols = expand(skip_gain)
    block_count = SEQUENCE_LENGTH // TOK_DEV

    def split_blocks(array):
        return array.reshape((block_count, TOK_DEV) + array.shape[1:])

    def one_sequence(pieces):
        values_seq, gate_seq, key_seq, query_seq, rate_seq, start_seq, grad_seq = pieces

        def forward(state_in, parts):
            values_in, key_block, query_block, step_block, doc_start = parts
            cumulative, weight_in, weight_start, weight_out, through, exit_start = tables(step_block, doc_start)
            mixing_block = make_mixing(key_block, query_block, cumulative, doc_start)
            values_heads = values_in.reshape(TOK_DEV, -1, HEAD_DIM).astype(jnp.float32)
            within = jnp.einsum('hts,shp->thp', mixing_block.astype(jnp.float32), values_heads).reshape(TOK_DEV, INNER)
            from_state = jnp.dot(query_block, state_in.astype(jnp.bfloat16), preferred_element_type=jnp.float32)
            from_start = jnp.dot(query_block, start_low, preferred_element_type=jnp.float32)
            ssd_out = (within + expand(weight_in) * from_state + expand(weight_start) * from_start + skip_cols * values_in.astype(jnp.float32)).astype(jnp.bfloat16)
            keys_weighted = weigh(weight_out, key_block)
            block_sum = jnp.einsum('hsn,shp->nhp', keys_weighted.astype(jnp.float32), values_heads).reshape(STATE, INNER)
            state_out = expand(through) * state_in + block_sum + expand(exit_start) * start_field
            return (state_out, ssd_out)
        forward_parts = (split_blocks(values_seq), split_blocks(key_seq), split_blocks(query_seq), split_blocks(rate_seq), start_seq)
        unused_state, ssd_all = lax.scan(forward, start_field, forward_parts)

        def backward(next_adjoint, parts):
            values_in, gate_block, key_block, query_block, step_block, doc_start, grad_block, ssd_out = parts
            silu_gate, silu_slope = silu_parts(gate_block.astype(jnp.float32))
            gated_value = ssd_out.astype(jnp.float32) * silu_gate
            inv_rms = lax.rsqrt(lax.optimization_barrier(jnp.sum(gated_value * gated_value, axis=1)) / INNER + EPSILON)
            normed = (gated_value * inv_rms[:, None] * norm_gain).astype(jnp.bfloat16)
            scaled = grad_block.astype(jnp.float32) * norm_gain
            inner_sum = lax.optimization_barrier(jnp.sum(scaled * gated_value, axis=1))
            gated_grad = inv_rms[:, None] * scaled - gated_value * (inner_sum * inv_rms ** 3 / INNER)[:, None]
            ssd_grad = (gated_grad * silu_gate).astype(jnp.bfloat16)
            grad_gate = (gated_grad * ssd_out.astype(jnp.float32) * silu_slope).astype(jnp.bfloat16)
            cumulative, weight_in, weight_start, weight_out, through, exit_start = tables(step_block, doc_start)
            mixing_block = make_mixing(key_block, query_block, cumulative, doc_start)
            grads_heads = ssd_grad.reshape(TOK_DEV, -1, HEAD_DIM).astype(jnp.float32)
            within_back = jnp.einsum('hts,thp->shp', mixing_block.astype(jnp.float32), grads_heads).reshape(TOK_DEV, INNER)
            from_next = jnp.dot(key_block, next_adjoint.astype(jnp.bfloat16), preferred_element_type=jnp.float32)
            grad_in = (within_back + expand(weight_out) * from_next + skip_cols * ssd_grad.astype(jnp.float32)).astype(jnp.bfloat16)
            query_in = weigh(weight_in, query_block).astype(jnp.float32)
            query_start = weigh(weight_start, query_block).astype(jnp.float32)
            visit_sum = jnp.einsum('htn,thp->nhp', query_in, grads_heads).reshape(STATE, INNER)
            reach_sum = jnp.einsum('htn,thp->nhp', query_start, grads_heads).reshape(STATE, INNER)
            adjoint_in = visit_sum + expand(through) * next_adjoint
            to_start = reach_sum + expand(exit_start) * next_adjoint
            return (adjoint_in, (normed, grad_in, grad_gate, to_start))
        backward_parts = (split_blocks(values_seq), split_blocks(gate_seq), split_blocks(key_seq), split_blocks(query_seq), split_blocks(rate_seq), start_seq, split_blocks(grad_seq), ssd_all)
        first_adjoint, outputs = lax.scan(backward, jnp.zeros((STATE, INNER), jnp.float32), backward_parts, reverse=True)
        normed, grad_in, grad_gate, to_start = outputs
        sequence_total = first_adjoint + lax.optimization_barrier(jnp.sum(to_start, axis=0))
        return (normed.reshape(SEQUENCE_LENGTH, INNER), grad_in.reshape(SEQUENCE_LENGTH, INNER), grad_gate.reshape(SEQUENCE_LENGTH, INNER), sequence_total)
    normed, grad_in, grad_gate, totals = lax.map(one_sequence, (seq_in, gate_in, keys_in, queries_in, step_rate, doc_starts, out_grad))
    start_total = lax.optimization_barrier(jnp.sum(totals, axis=0))
    grad_prompt, grad_start = derive(start_total, prompt_keys, weight_cols, carry_cols)
    return (normed, grad_in, grad_gate, grad_prompt, grad_start)
```

```python
import functools

import jax
import jax.numpy as jnp
from jax import lax
from jax.experimental import pallas as pl
from jax.experimental.pallas import tpu as pltpu
from jax.sharding import PartitionSpec as P

HEAD_DIM = 64
EPSILON = 1e-05
LANES = 128
GROUP = 8
LANE_IN, LANE_START, LANE_OUT = GROUP, 2 * GROUP, 3 * GROUP
EXTRA = 8
ROWS = 128

F32 = jnp.float32
BF16 = jnp.bfloat16
EXACT = lax.Precision.HIGHEST


def iota(shape, dim):
    return lax.broadcasted_iota(jnp.int32, shape, dim)


def mm(a, b, da=1, db=0, precision=None):
    return lax.dot_general(
        a, b, (((da,), (db,)), ((), ())), precision=precision, preferred_element_type=F32
    )


def two_heads(table, first):
    rows = table.shape[0]
    left = jnp.broadcast_to(table[:, first : first + 1], (rows, LANES))
    right = jnp.broadcast_to(table[:, first + 1 : first + 2], (rows, LANES))
    return jnp.where(iota((rows, LANES), 1) < HEAD_DIM, left, right)


def tile(p):
    return slice(p * LANES, (p + 1) * LANES)


def row_block(i):
    return slice(i * ROWS, (i + 1) * ROWS)


def call(kernel, outs, ins, out_shapes, scratch=(), alias=None, flops=10**7, limit=24):
    moved = sum(s.size * s.dtype.itemsize for s in out_shapes)
    return pl.pallas_call(
        kernel,
        grid=(1,),
        in_specs=ins,
        out_specs=outs,
        out_shape=out_shapes,
        scratch_shapes=list(scratch),
        input_output_aliases=alias or {},
        cost_estimate=pl.CostEstimate(flops=flops, bytes_accessed=moved, transcendentals=0),
        compiler_params=pltpu.CompilerParams(vmem_limit_bytes=limit * 2**20),
    )


def whole(array):
    zeros = (0,) * array.ndim
    return pl.BlockSpec(array.shape, lambda s: zeros)


def columns(array, k, width):
    lead = (0,) * (array.ndim - 1)
    return pl.BlockSpec(array.shape[:-1] + (width,), lambda s: lead + (k,))


SCALAR = pl.BlockSpec(memory_space=pltpu.SMEM)
ANYWHERE = pl.BlockSpec(memory_space=pl.ANY)


def silu(value):
    sigmoid = 1.0 / (1.0 + jnp.exp(-value))
    return value * sigmoid, sigmoid


def open_kernel(
    k, doc, step_ref, keys, seq, prompt_in, prompt_keys, rate, state,
    tab_ref, first_ref, move_ref, start_ref, cols_ref, weighted,
):
    rows, heads = step_ref.shape
    doc_start = doc[0, 0]
    step = step_ref[...]
    hh, ll = iota((heads, LANES), 0), iota((heads, LANES), 1)
    spread = jnp.where((ll < 4 * GROUP) & (hh == k * GROUP + (ll & (GROUP - 1))), 1.0, 0.0)
    spread = spread.astype(BF16)
    tri = jnp.where(iota((rows, rows), 0) >= iota((rows, rows), 1), 1.0, 0.0).astype(BF16)
    high = step.astype(BF16)
    rest = step - high.astype(F32)
    middle = rest.astype(BF16)
    low = (rest - middle.astype(F32)).astype(BF16)
    step_rep = jnp.zeros((rows, LANES), F32)
    cum = jnp.zeros((rows, LANES), F32)
    for part in (low, middle, high):
        rep = mm(part, spread)
        step_rep = step_rep + rep
        cum = cum + mm(tri, rep.astype(BF16))
    before = cum - step_rep
    pos = iota((rows, LANES), 0)
    kind = iota((rows, LANES), 1) // GROUP
    has = doc_start < rows
    ex_start = jnp.sum(jnp.where(pos == doc_start, before, 0.0), axis=0, keepdims=True)
    end = cum[rows - 1 : rows]
    arg = jnp.where(kind == 1, -cum, jnp.where(kind == 2, ex_start - cum, cum - end))
    tail_start = jnp.where(has, doc_start, 0)
    keep = (
        ((kind == 1) & (pos < doc_start))
        | ((kind == 2) & (pos >= doc_start))
        | ((kind == 3) & (pos >= tail_start))
    )
    weights = jnp.where(keep, jnp.exp(jnp.minimum(arg, 0.0)), 0.0)
    tab = jnp.where(kind == 0, cum, weights)
    tab_ref[...] = tab
    through = jnp.where(has, 0.0, jnp.exp(-end))
    leave = jnp.where(has, jnp.exp(ex_start - end), 0.0)

    suffix_mask = jnp.where(iota((rate.shape[0],) * 2, 0) < iota((rate.shape[0],) * 2, 1), 1.0, 0.0)
    suffix = mm(suffix_mask, rate[...], precision=EXACT)
    spread_weight = jnp.exp(-suffix)
    carry = jnp.exp(-jnp.sum(rate[...], axis=0, keepdims=True))
    prompt_rows = rate.shape[0]
    for p in range(GROUP // 2):
        cols_ref[:prompt_rows, tile(p)] = two_heads(spread_weight, k * GROUP + 2 * p)
        cols_ref[prompt_rows : prompt_rows + 8, tile(p)] = jnp.broadcast_to(
            two_heads(carry, k * GROUP + 2 * p), (8, LANES)
        )
        cols_ref[prompt_rows + 8 : prompt_rows + 16, tile(p)] = jnp.broadcast_to(
            two_heads(through, 2 * p), (8, LANES)
        )
        cols_ref[prompt_rows + 16 : prompt_rows + 24, tile(p)] = jnp.broadcast_to(
            two_heads(leave, 2 * p), (8, LANES)
        )
        values = seq[0, :, tile(p)].astype(F32)
        weighted[:, tile(p)] = (values * two_heads(tab, LANE_OUT + 2 * p)).astype(BF16)
    state_rows = state.shape[0]
    field = mm(
        prompt_keys[...].astype(F32), cols_ref[:prompt_rows] * prompt_in[...].astype(F32), 0, 0, EXACT
    )
    start = field + cols_ref[prompt_rows : prompt_rows + 1] * state[...]
    through_cols = cols_ref[prompt_rows + 8 : prompt_rows + 9]
    leave_cols = cols_ref[prompt_rows + 16 : prompt_rows + 17]
    move = mm(keys[0], weighted[...], 0, 0) + leave_cols * start
    start_ref[:state_rows] = start
    move_ref[:state_rows] = move
    first_ref[:state_rows] = through_cols * start + move
    start_ref[state_rows:] = jnp.ones((EXTRA, start.shape[1]), F32)
    extra = jnp.broadcast_to(leave_cols, (EXTRA, start.shape[1]))
    move_ref[state_rows:] = extra
    first_ref[state_rows:] = through_cols + extra


def within_kernel(k, doc, tab_ref, keys, queries, seq, start, skip, order, base_ref):
    del order
    rows = tab_ref.shape[0]
    state_rows = keys.shape[2]
    doc_start = doc[0, 0]
    lane = iota((1, LANES), 1)
    halves = [jnp.where(lane < HEAD_DIM, 1.0, 0.0).astype(BF16), jnp.where(lane >= HEAD_DIM, 1.0, 0.0).astype(BF16)]
    cum_rows = jnp.transpose(tab_ref[...])
    from_start = mm(queries[0], start[:state_rows].astype(BF16))
    values = [[seq[0, :, tile(p)] * half for half in halves] for p in range(GROUP // 2)]
    for i in range(rows // ROWS):
        upto = (i + 1) * ROWS
        scores = mm(queries[0, row_block(i)], keys[0, :upto], 1, 1)
        t = iota((ROWS, upto), 0) + i * ROWS
        s = iota((ROWS, upto), 1)
        same = (s <= t) & ((t < doc_start) | (s >= doc_start))
        scores = jnp.where(same, scores, 0.0)
        tab = tab_ref[row_block(i)]
        for p in range(GROUP // 2):
            total = two_heads(tab, LANE_START + 2 * p) * from_start[row_block(i), tile(p)]
            total += two_heads(skip[...], k * GROUP + 2 * p) * seq[0, row_block(i), tile(p)].astype(F32)
            for half in range(2):
                h = 2 * p + half
                gap = cum_rows[h : h + 1, :upto] - tab[:, h : h + 1]
                mixing = (scores * jnp.exp(jnp.minimum(gap, 0.0))).astype(BF16)
                total += mm(mixing, values[p][half][:upto])
            base_ref[row_block(i), tile(p)] = total


def gate_kernel(tab_ref, base, state_in, queries, gate, grad, gain, before, out_ref, stat_ref):
    rows = tab_ref.shape[0]
    state_rows = queries.shape[2]
    reads = mm(queries[0], state_in[:state_rows].astype(BF16))
    for i in range(rows // ROWS):
        rb = row_block(i)
        tab = tab_ref[rb]
        squares = jnp.zeros((ROWS, LANES), F32)
        inner = jnp.zeros((ROWS, LANES), F32)
        for p in range(GROUP // 2):
            out = (base[rb, tile(p)] + two_heads(tab, LANE_IN + 2 * p) * reads[rb, tile(p)]).astype(BF16)
            out_ref[rb, tile(p)] = out
            act, _ = silu(gate[0, rb, tile(p)].astype(F32))
            gated = out.astype(F32) * act
            squares += gated * gated
            inner += grad[0, rb, tile(p)].astype(F32) * gain[:, tile(p)] * gated
        lane = iota((ROWS, 8), 1)
        sums = jnp.where(
            lane == 0,
            jnp.sum(squares, axis=1, keepdims=True),
            jnp.where(lane == 1, jnp.sum(inner, axis=1, keepdims=True), 0.0),
        )
        stat_ref[rb] = sums if before is None else before[rb] + sums


def norm_factors(inner_cols, stat):
    inverse = lax.rsqrt(stat[:, 0:1] / inner_cols + EPSILON)
    pull = stat[:, 1:2] * inverse * inverse * inverse / inner_cols
    return inverse, pull


def visit_kernel(
    inner_cols, tab_ref, stat_a, stat_b, out, gate, grad, gain, queries, state_in, *rest
):
    ssd_ref, visit_ref, part_ref, into, begun = rest[-5:]
    rows = tab_ref.shape[0]
    state_rows = queries.shape[2]
    for i in range(rows // ROWS):
        rb = row_block(i)
        tab = tab_ref[rb]
        inverse, pull = norm_factors(inner_cols, stat_a[rb] + stat_b[rb])
        for p in range(GROUP // 2):
            act, _ = silu(gate[0, rb, tile(p)].astype(F32))
            gated = out[rb, tile(p)].astype(F32) * act
            scaled = grad[0, rb, tile(p)].astype(F32) * gain[:, tile(p)]
            ssd = ((inverse * scaled - gated * pull) * act).astype(BF16)
            ssd_ref[rb, tile(p)] = ssd
            wide = ssd.astype(F32)
            into[rb, tile(p)] = (two_heads(tab, LANE_IN + 2 * p) * wide).astype(BF16)
            begun[rb, tile(p)] = (two_heads(tab, LANE_START + 2 * p) * wide).astype(BF16)
    visit = mm(queries[0], into[...], 0, 0)
    visit_ref[...] = visit
    part_ref[...] = mm(queries[0], begun[...], 0, 0) + state_in[state_rows : state_rows + 1] * visit


def back_kernel(
    k, inner_cols, doc, tab_ref, keys, queries, stat_a, stat_b, out, gate, grad, gain, ssd_grad, skip, *rest
):
    base_ref, normed_ref, gate_grad_ref = rest[-3:]
    rows = tab_ref.shape[0]
    doc_start = doc[0, 0]
    lane = iota((1, LANES), 1)
    halves = [jnp.where(lane < HEAD_DIM, 1.0, 0.0).astype(BF16), jnp.where(lane >= HEAD_DIM, 1.0, 0.0).astype(BF16)]
    cum_rows = jnp.transpose(tab_ref[...])
    grads = [[ssd_grad[:, tile(p)] * half for half in halves] for p in range(GROUP // 2)]
    for i in range(rows // ROWS):
        rb = row_block(i)
        down = i * ROWS
        scores = mm(keys[0, rb], queries[0, down:], 1, 1)
        s = iota((ROWS, rows - down), 0) + down
        t = iota((ROWS, rows - down), 1) + down
        same = (s <= t) & ((t < doc_start) | (s >= doc_start))
        scores = jnp.where(same, scores, 0.0)
        tab = tab_ref[rb]
        inverse, pull = norm_factors(inner_cols, stat_a[rb] + stat_b[rb])
        for p in range(GROUP // 2):
            wide = ssd_grad[rb, tile(p)].astype(F32)
            total = two_heads(skip[...], k * GROUP + 2 * p) * wide
            for half in range(2):
                h = 2 * p + half
                gap = tab[:, h : h + 1] - cum_rows[h : h + 1, down:]
                mixing = (scores * jnp.exp(jnp.minimum(gap, 0.0))).astype(BF16)
                total += mm(mixing, grads[p][half][down:])
            base_ref[rb, tile(p)] = total
            value = gate[0, rb, tile(p)].astype(F32)
            act, sigmoid = silu(value)
            slope = sigmoid * (1.0 + value * (1.0 - sigmoid))
            wide_out = out[rb, tile(p)].astype(F32)
            gated = wide_out * act
            gains = gain[:, tile(p)]
            scaled = grad[0, rb, tile(p)].astype(F32) * gains
            normed_ref[0, rb, tile(p)] = (gated * inverse * gains).astype(BF16)
            gated_grad = inverse * scaled - gated * pull
            gate_grad_ref[0, rb, tile(p)] = (gated_grad * wide_out * slope).astype(BF16)


def close_kernel(tab_ref, base, adjoint, keys, *rest):
    grad_ref = rest[-1]
    rows = tab_ref.shape[0]
    reads = mm(keys[0], adjoint[...].astype(BF16))
    for i in range(rows // ROWS):
        rb = row_block(i)
        tab = tab_ref[rb]
        for p in range(GROUP // 2):
            grad_ref[0, rb, tile(p)] = (
                base[rb, tile(p)] + two_heads(tab, LANE_OUT + 2 * p) * reads[rb, tile(p)]
            ).astype(BF16)


def derive_kernel(chunks, total, prompt_keys, *rest):
    cols, (prompt_ref, start_ref) = rest[:chunks], rest[chunks:]
    prompt_rows = prompt_keys.shape[0]
    keys = prompt_keys[...].astype(F32)
    for k in range(chunks):
        width = cols[k].shape[1]
        span = slice(k * width, (k + 1) * width)
        grads = total[:, span]
        start_ref[:, span] = cols[k][prompt_rows : prompt_rows + 1] * grads
        prompt_ref[:, span] = cols[k][:prompt_rows] * mm(keys, grads, precision=EXACT)


def swap(array, bit):
    count = lax.axis_size("dp")
    return lax.ppermute(array, "dp", [(i, i ^ bit) for i in range(count)])


def pick(array, index, axis):
    return lax.dynamic_index_in_dim(array, index, axis, keepdims=False)


def ordered(flag, mine, other, axis):
    return jnp.where(flag == 0, jnp.stack([mine, other], axis), jnp.stack([other, mine], axis))


def sum_blocks(part):
    place = lax.axis_index("dp")
    low, high = place & 1, place >> 1
    span = part.shape[0] // 8
    width = part.shape[1]
    part = part.reshape(2, 2, 2, span, width)
    one, two = part[0], part[1]
    one = pick(one, low, 1) + swap(pick(one, 1 - low, 1), 1)
    two = pick(two, high, 0) + swap(pick(two, 1 - high, 0), 2)
    one = pick(one, high, 0) + swap(pick(one, 1 - high, 0), 2)
    two = pick(two, low, 0) + swap(pick(two, 1 - low, 0), 1)

    count = lax.axis_size("ctx")
    here = lax.axis_index("ctx")
    both = jnp.concatenate([one, two], 0).reshape(count, 2 * span // count, width)
    shifts = range(1, count)
    ring = [[(i, (i + d) % count) for i in range(count)] for d in range(count)]
    total = pick(both, here, 0)
    for d in shifts:
        total = total + lax.ppermute(pick(both, (here + d) % count, 0), "ctx", ring[d])
    gathered = lax.dynamic_update_index_in_dim(jnp.zeros_like(both), total, here, 0)
    for d in shifts:
        arrived = lax.ppermute(total, "ctx", ring[d])
        gathered = lax.dynamic_update_index_in_dim(gathered, arrived, (here - d) % count, 0)
    both = gathered.reshape(2, span, width)

    one, two = both[0], both[1]
    one = ordered(high, one, swap(one, 2), 0)
    two = ordered(low, two, swap(two, 1), 0)
    one = ordered(low, one, swap(one, 1), 1)
    two = ordered(high, two, swap(two, 2), 0)
    return jnp.concatenate([one.reshape(4 * span, width), two.reshape(4 * span, width)], 0)


def shape(*dims, dtype=F32):
    return jax.ShapeDtypeStruct(dims, dtype)


def body(
    seq_in,
    gate_in,
    keys_in,
    queries_in,
    step_rate,
    doc_starts,
    skip_gain,
    norm_gain,
    prompt_in,
    prompt_keys,
    prompt_rate,
    start_state,
    out_grad,
):
    _, rows, cols = seq_in.shape
    state_rows = keys_in.shape[2]
    heads = step_rate.shape[2]
    prompt_rows = prompt_in.shape[0]
    chunks = heads // GROUP
    width = cols // chunks
    inner_cols = cols * lax.axis_size("tensor")
    count = lax.axis_size("ctx")
    first_block = lax.axis_index("ctx") == 0
    step = step_rate.reshape(rows, heads)
    skip = skip_gain.reshape(1, heads)
    gain = norm_gain.reshape(1, cols)
    each = range(chunks)
    message = shape(state_rows + EXTRA, width)

    def blocked(array, k):
        return columns(array, k, width)

    tabs, firsts, moves, starts, col_tabs = [], [], [], [], []
    for k in each:
        tab, first, move, start, col_tab = call(
            functools.partial(open_kernel, k),
            [whole(s) for s in (shape(rows, LANES), message, message, message, shape(prompt_rows + 24, width))],
            [
                SCALAR,
                whole(step),
                whole(keys_in),
                blocked(seq_in, k),
                blocked(prompt_in, k),
                whole(prompt_keys),
                whole(prompt_rate),
                blocked(start_state, k),
            ],
            [shape(rows, LANES), message, message, message, shape(prompt_rows + 24, width)],
            [pltpu.VMEM((rows, width), BF16)],
        )(doc_starts, step, keys_in, seq_in, prompt_in, prompt_keys, prompt_rate, start_state)
        tabs.append(tab)
        firsts.append(first)
        moves.append(move)
        starts.append(start)
        col_tabs.append(col_tab)
    through = [c[prompt_rows + 8 : prompt_rows + 9] for c in col_tabs]

    states = [jnp.where(first_block, s, 0.0) for s in starts]
    bases = [None] * chunks
    for edge in range(count - 1):
        for k in each:
            send = firsts[k] if edge == 0 else through[k] * states[k] + moves[k]
            arrived = lax.ppermute(send, "ctx", [(edge, edge + 1)])
            states[k] = states[k] + arrived
    for k in each:
        (bases[k],) = call(
            functools.partial(within_kernel, k),
            [whole(shape(rows, width))],
            [
                SCALAR,
                whole(tabs[k]),
                whole(keys_in),
                whole(queries_in),
                blocked(seq_in, k),
                whole(starts[k]),
                whole(skip),
                ANYWHERE,
            ],
            [shape(rows, width)],
            flops=3 * 10**9,
        )(doc_starts, tabs[k], keys_in, queries_in, seq_in, starts[k], skip, starts[k])

    outs, stat = [], None
    for k in each:
        operands = [tabs[k], bases[k], states[k], queries_in, gate_in, out_grad, gain]
        specs = [
            whole(tabs[k]),
            whole(bases[k]),
            whole(states[k]),
            whole(queries_in),
            blocked(gate_in, k),
            blocked(out_grad, k),
            blocked(gain, k),
        ]
        kernel = gate_kernel
        if stat is None:
            kernel = lambda *refs: gate_kernel(*refs[:7], None, *refs[7:])
        else:
            operands.append(stat)
            specs.append(whole(stat))
        out, stat = call(
            kernel,
            [whole(shape(rows, width)), whole(shape(rows, 8))],
            specs,
            [shape(rows, width, dtype=BF16), shape(rows, 8)],
        )(*operands)
        outs.append(out)
    pairs = [(i, (i + 1) % lax.axis_size("tensor")) for i in range(lax.axis_size("tensor"))]
    stat_other = lax.ppermute(stat, "tensor", pairs)

    ssd_grads, visits, part = [], [], None
    for k in each:
        operands = [tabs[k], stat, stat_other, outs[k], gate_in, out_grad, gain, queries_in, states[k]]
        specs = [
            whole(tabs[k]),
            whole(stat),
            whole(stat),
            whole(outs[k]),
            blocked(gate_in, k),
            blocked(out_grad, k),
            blocked(gain, k),
            whole(queries_in),
            whole(states[k]),
        ]
        alias = {}
        if part is not None:
            operands.append(part)
            specs.append(ANYWHERE)
            alias = {len(operands) - 1: 2}
        part_shape = shape(state_rows, cols)
        ssd, visit, part = call(
            functools.partial(visit_kernel, inner_cols),
            [whole(shape(rows, width)), whole(shape(state_rows, width)), blocked(part_shape, k)],
            specs,
            [shape(rows, width, dtype=BF16), shape(state_rows, width), part_shape],
            [pltpu.VMEM((rows, width), BF16)] * 2,
            alias,
        )(*operands)
        ssd_grads.append(ssd)
        visits.append(visit)

    adjoints = [jnp.zeros((state_rows, width), F32) for k in each]
    for edge in range(count - 1, 0, -1):
        for k in each:
            send = visits[k] if edge == count - 1 else visits[k] + through[k] * adjoints[k]
            adjoints[k] = adjoints[k] + lax.ppermute(send, "ctx", [(edge, edge - 1)])

    total = sum_blocks(part)

    back_bases = [None] * chunks
    normed = gate_grad = None
    for k in each:
        operands = [
            doc_starts, tabs[k], keys_in, queries_in, stat, stat_other, outs[k], gate_in, out_grad, gain, ssd_grads[k], skip,
        ]
        specs = [
            SCALAR,
            whole(tabs[k]),
            whole(keys_in),
            whole(queries_in),
            whole(stat),
            whole(stat),
            whole(outs[k]),
            blocked(gate_in, k),
            blocked(out_grad, k),
            blocked(gain, k),
            whole(ssd_grads[k]),
            whole(skip),
        ]
        alias = {}
        if normed is not None:
            operands += [normed, gate_grad]
            specs += [ANYWHERE, ANYWHERE]
            alias = {len(operands) - 2: 1, len(operands) - 1: 2}
        full = shape(*seq_in.shape, dtype=BF16)
        back_bases[k], normed, gate_grad = call(
            functools.partial(back_kernel, k, inner_cols),
            [whole(shape(rows, width)), blocked(full, k), blocked(full, k)],
            specs,
            [shape(rows, width), full, full],
            alias=alias,
            flops=3 * 10**9,
        )(*operands)

    grad_in = None
    for k in each:
        operands = [tabs[k], back_bases[k], adjoints[k], keys_in]
        specs = [whole(tabs[k]), whole(back_bases[k]), whole(adjoints[k]), whole(keys_in)]
        alias = {}
        if grad_in is not None:
            operands.append(grad_in)
            specs.append(ANYWHERE)
            alias = {len(operands) - 1: 0}
        full = shape(*seq_in.shape, dtype=BF16)
        (grad_in,) = call(close_kernel, [blocked(full, k)], specs, [full], alias=alias)(*operands)

    out_shapes = [shape(prompt_rows, cols), shape(state_rows, cols)]
    grad_prompt, grad_start = call(
        functools.partial(derive_kernel, chunks),
        [whole(s) for s in out_shapes],
        [whole(total), whole(prompt_keys)] + [whole(c) for c in col_tabs],
        out_shapes,
    )(total, prompt_keys, *col_tabs)
    return normed, grad_in, gate_grad, grad_prompt, grad_start


def solution(mesh):
    return jax.shard_map(
        body,
        mesh=mesh,
        in_specs=(
            P("dp", "ctx", "tensor"),
            P("dp", "ctx", "tensor"),
            P("dp", "ctx", None),
            P("dp", "ctx", None),
            P("dp", "ctx", "tensor"),
            P("dp", "ctx"),
            P("tensor"),
            P("tensor"),
            P(None, "tensor"),
            P(),
            P(None, "tensor"),
            P(None, "tensor"),
            P("dp", "ctx", "tensor"),
        ),
        out_specs=(
            P("dp", "ctx", "tensor"),
            P("dp", "ctx", "tensor"),
            P("dp", "ctx", "tensor"),
            P(None, "tensor"),
            P(None, "tensor"),
        ),
        check_vma=False,
    )
```

```python
import functools

import jax
import jax.numpy as jnp
from jax import lax
from jax.experimental import pallas as pl
from jax.experimental.pallas import tpu as pltpu
from jax.sharding import PartitionSpec as P

HEAD_DIM = 64
EPSILON = 1e-05
LANES = 128
VLIM = 32
PLIM = 60
GROUP = 8
KIND_IN, KIND_OUT = 1, 3
EXTRA = 8
ROWS = 128

F32 = jnp.float32
BF16 = jnp.bfloat16
EXACT = lax.Precision.HIGHEST


def iota(shape, dim):
    return lax.broadcasted_iota(jnp.int32, shape, dim)


def mm(a, b, da=1, db=0, precision=None):
    return lax.dot_general(
        a, b, (((da,), (db,)), ((), ())), precision=precision, preferred_element_type=F32
    )


def two_heads(table, first):
    rows = table.shape[0]
    left = jnp.broadcast_to(table[:, first : first + 1], (rows, LANES))
    right = jnp.broadcast_to(table[:, first + 1 : first + 2], (rows, LANES))
    return jnp.where(iota((rows, LANES), 1) < HEAD_DIM, left, right)


def spread_weights(wide, kind, width):
    lane, col = iota((LANES, width), 0), iota((LANES, width), 1)
    part = lane // GROUP
    hit = ((part == kind) | (part == kind + 1)) & ((lane & (GROUP - 1)) == col // HEAD_DIM)
    return mm(wide, jnp.where(hit, 1.0, 0.0).astype(BF16))


def split_queries(queries, doc_start):
    rows, width = queries.shape
    ahead = iota((rows, width), 0) < doc_start
    wide = queries.astype(F32)
    both = [jnp.where(ahead, wide, 0.0), jnp.where(ahead, 0.0, wide)]
    return jnp.concatenate(both, axis=1).astype(BF16)


def tile(p):
    return slice(p * LANES, (p + 1) * LANES)


def row_block(i):
    return slice(i * ROWS, (i + 1) * ROWS)


def call(kernel, outs, ins, out_shapes, scratch=(), alias=None, limit=16, steps=1):
    return pl.pallas_call(
        kernel,
        grid=(steps,),
        in_specs=ins,
        out_specs=outs,
        out_shape=out_shapes,
        scratch_shapes=list(scratch),
        input_output_aliases=alias or {},
        cost_estimate=pl.CostEstimate(flops=0, bytes_accessed=0, transcendentals=0),
        compiler_params=pltpu.CompilerParams(vmem_limit_bytes=limit * 2**20),
    )


def whole(array):
    zeros = (0,) * array.ndim
    return pl.BlockSpec(array.shape, lambda s: zeros)


def columns(array, k, width):
    lead = (0,) * (array.ndim - 1)
    return pl.BlockSpec(array.shape[:-1] + (width,), lambda s: lead + (k,))


SCALAR = pl.BlockSpec(memory_space=pltpu.SMEM)
ANYWHERE = pl.BlockSpec(memory_space=pl.ANY)


def silu(value):
    sigmoid = 0.5 + 0.5 * jnp.tanh(0.5 * value)
    return value * sigmoid, sigmoid


def open_kernel(
    k, doc, step_ref, keys, seq, prompt_in, prompt_keys, rate, state,
    tab_ref, wide_ref, first_ref, move_ref, late_ref, mine_ref, through_ref, low_ref, cols_ref,
):
    heads, rows = step_ref.shape[1:]
    doc_start = doc[0, 0]
    step = step_ref[0]
    hh, ll = iota((heads, LANES), 0), iota((heads, LANES), 1)
    spread = jnp.where((ll < 5 * GROUP) & (hh == k * GROUP + (ll & (GROUP - 1))), 1.0, 0.0)
    spread = spread.astype(BF16)
    tri = jnp.where(iota((rows, rows), 0) >= iota((rows, rows), 1), 1.0, 0.0).astype(BF16)
    high = step.astype(BF16)
    rest = step - high.astype(F32)
    middle = rest.astype(BF16)
    low = (rest - middle.astype(F32)).astype(BF16)
    step_rep = jnp.zeros((rows, LANES), F32)
    cum = jnp.zeros((rows, LANES), F32)
    for part in (low, middle, high):
        rep = mm(part, spread, 0, 0)
        step_rep = step_rep + rep
        cum = cum + mm(tri, rep.astype(BF16))
    before = cum - step_rep
    pos = iota((rows, LANES), 0)
    kind = iota((rows, LANES), 1) // GROUP
    has = doc_start < rows
    ex_start = jnp.sum(jnp.where(pos == doc_start, before, 0.0), axis=0, keepdims=True)
    end = cum[rows - 1 : rows]
    tail_start = jnp.where(has, doc_start, 0)
    arg = jnp.where(kind < KIND_OUT, jnp.where(pos < doc_start, 0.0, ex_start) - cum, cum - end)
    keep = (kind < KIND_OUT) | (pos >= tail_start)
    weights = jnp.where(keep, jnp.exp(jnp.minimum(arg, 0.0)), 0.0)
    tab_ref[...] = cum
    head_part = weights.astype(BF16).astype(F32)
    is_head = (kind == KIND_IN) | (kind == KIND_OUT)
    wide = jnp.where(is_head, head_part, weights - head_part).astype(BF16)
    wide_ref[...] = wide
    through = jnp.where(has, 0.0, jnp.exp(-end))
    leave = jnp.where(has, jnp.exp(ex_start - end), 0.0)

    prompt_rows = rate.shape[0]
    square = (prompt_rows, prompt_rows)
    later = jnp.where(iota(square, 0) < iota(square, 1), 1.0, 0.0)
    spread_weight = jnp.exp(-mm(later, rate[...], precision=EXACT))
    carry = jnp.exp(-jnp.sum(rate[...], axis=0, keepdims=True))
    for p in range(GROUP // 2):
        cols_ref[:prompt_rows, tile(p)] = two_heads(spread_weight, k * GROUP + 2 * p)
        for place, row in ((0, two_heads(carry, k * GROUP + 2 * p)), (8, two_heads(through, 2 * p))):
            rows_here = slice(prompt_rows + place, prompt_rows + place + 8)
            cols_ref[rows_here, tile(p)] = jnp.broadcast_to(row, (8, LANES))
        cols_ref[prompt_rows + 16 : prompt_rows + 24, tile(p)] = jnp.broadcast_to(
            two_heads(leave, 2 * p), (8, LANES)
        )
    state_rows, width = state.shape
    weighted = (seq[0].astype(F32) * spread_weights(wide, KIND_OUT, width)).astype(BF16)
    field = mm(
        prompt_keys[...].astype(F32), cols_ref[:prompt_rows] * prompt_in[...].astype(F32), 0, 0, EXACT
    )
    start = field + cols_ref[prompt_rows : prompt_rows + 1] * state[...]
    through_cols = cols_ref[prompt_rows + 8 : prompt_rows + 9]
    through_ref[...] = jnp.broadcast_to(through_cols, through_ref.shape)
    leave_cols = cols_ref[prompt_rows + 16 : prompt_rows + 17]
    move = mm(keys[0], weighted, 0, 0) + leave_cols * start
    is_first = lax.axis_index("ctx") == 0
    low_ref[...] = start.astype(BF16)
    mine_ref[:state_rows] = jnp.where(is_first, start, 0.0)
    move_ref[:state_rows] = move
    late_ref[:state_rows] = move
    first_ref[:state_rows] = through_cols * start + move
    ones = jnp.ones((EXTRA, width), F32)
    mine_ref[state_rows:] = jnp.where(is_first, ones, 0.0)
    extra = jnp.broadcast_to(leave_cols, (EXTRA, width))
    move_ref[state_rows:] = extra
    late_ref[state_rows:] = extra
    first_ref[state_rows:] = through_cols + extra


def open_from_hbm(ks, cut, outs, doc, *refs):
    ins = len(cut)
    held, buffers, sems = refs[:ins], refs[-1 - ins : -1], refs[-1]
    made = refs[-1 - ins - outs * len(ks) : -1 - ins]
    copies = []
    for n, (source, buffer) in enumerate(zip(held, buffers)):
        width = buffer.shape[-1]
        columns_here = pl.ds(ks[0] * (width // len(ks)) if cut[n] else 0, width)
        lead = (slice(None),) * (len(buffer.shape) - 1)
        copies.append(pltpu.make_async_copy(source.at[lead + (columns_here,)], buffer, sems.at[n]))
    for copy in copies:
        copy.start()
    for copy in copies:
        copy.wait()
    for place, k in enumerate(ks):
        mine = []
        for buffer, is_cut in zip(buffers, cut):
            width = buffer.shape[-1] // len(ks)
            lead = (slice(None),) * (len(buffer.shape) - 1)
            mine.append(buffer.at[lead + (pl.ds(place * width, width),)] if is_cut else buffer)
        open_kernel(k, doc, *mine, *made[place * outs : (place + 1) * outs])


def step_kernel(arrived, move, through, *rest):
    mine, (sum_ref, send_ref) = rest[:-2], rest[-2:]
    total = arrived[...] if not mine else mine[0][...] + arrived[...]
    sum_ref[...] = total
    send_ref[...] = through[: total.shape[0]] * total + move[...]


def head_halves():
    lane = iota((1, LANES), 1)
    return [jnp.where(half, 1.0, 0.0).astype(BF16) for half in (lane < HEAD_DIM, lane >= HEAD_DIM)]


def within_kernel(k, doc, tab_ref, keys, queries, seq, skip, base_ref):
    rows = tab_ref.shape[0]
    doc_start = doc[0, 0]
    halves = head_halves()
    cum_rows = jnp.transpose(tab_ref[...])
    values = [[seq[0, :, tile(p)] * half for half in halves] for p in range(GROUP // 2)]
    for i in range(rows // ROWS):
        upto = (i + 1) * ROWS
        scores = mm(queries[0, row_block(i)], keys[0, :upto], 1, 1)
        t = iota((ROWS, upto), 0) + i * ROWS
        s = iota((ROWS, upto), 1)
        same = (s <= t) & ((t < doc_start) | (s >= doc_start))
        scores = jnp.where(same, scores, 0.0)
        tab = tab_ref[row_block(i)]
        for p in range(GROUP // 2):
            total = two_heads(skip[...], k * GROUP + 2 * p) * seq[0, row_block(i), tile(p)].astype(F32)
            for half in range(2):
                h = 2 * p + half
                gap = cum_rows[h : h + 1, :upto] - tab[:, h : h + 1]
                mixing = (scores * jnp.exp(jnp.minimum(gap, 0.0))).astype(BF16)
                total += mm(mixing, values[p][half][:upto])
            base_ref[row_block(i), tile(p)] = total


def gate_kernel(
    doc, wide, base, mine, arrived, low, queries, gate, grad, gain, before, *rest
):
    out_ref, stat_ref, share_ref = rest[-3:]
    rows, width = base.shape
    state_rows = low.shape[0]
    state_in = mine[...] + arrived[...]
    share_ref[...] = state_in[state_rows:]
    fields = jnp.concatenate([state_in[:state_rows].astype(BF16), low[...]], axis=0)
    reads = mm(split_queries(queries[0], doc[0, 0]), fields)
    weights = spread_weights(wide[...], KIND_IN, width)
    for i in range(rows // ROWS):
        rb = row_block(i)
        squares = jnp.zeros((ROWS, LANES), F32)
        inner = jnp.zeros((ROWS, LANES), F32)
        for p in range(GROUP // 2):
            out = (base[rb, tile(p)] + weights[rb, tile(p)] * reads[rb, tile(p)]).astype(BF16)
            out_ref[rb, tile(p)] = out
            act, _ = silu(gate[0, rb, tile(p)].astype(F32))
            gated = out.astype(F32) * act
            squares += gated * gated
            inner += grad[0, rb, tile(p)].astype(F32) * gain[:, tile(p)] * gated
        lane = iota((ROWS, 8), 1)
        sums = jnp.where(
            lane == 0,
            jnp.sum(squares, axis=1, keepdims=True),
            jnp.where(lane == 1, jnp.sum(inner, axis=1, keepdims=True), 0.0),
        )
        stat_ref[rb] = sums if before is None else before[rb] + sums


def norm_factors(inner_cols, stat):
    inverse = lax.rsqrt(stat[:, 0:1] / inner_cols + EPSILON)
    pull = stat[:, 1:2] * inverse * inverse * inverse / inner_cols
    shape = (stat.shape[0], LANES)
    return jnp.broadcast_to(inverse, shape), jnp.broadcast_to(pull, shape)


def visit_kernel(
    inner_cols, chunks, doc, stat_a, stat_b, out, gate, grad, gain, queries, share, *rest
):
    wides, ssd_ref, weighted, part = rest[:chunks], rest[chunks], rest[-2], rest[-1]
    visits, parts = rest[chunks + 1 : 2 * chunks + 1], rest[2 * chunks + 1 : -2]
    wide = wides[0][...]
    for n in range(1, chunks):
        wide = jnp.where(pl.program_id(0) == n, wides[n][...], wide)
    rows, width = out.shape
    state_rows = queries.shape[2]
    weights = spread_weights(wide, KIND_IN, width)
    for i in range(rows // ROWS):
        rb = row_block(i)
        inverse, pull = norm_factors(inner_cols, stat_a[rb] + stat_b[rb])
        for p in range(GROUP // 2):
            act, _ = silu(gate[0, rb, tile(p)].astype(F32))
            gated = out[rb, tile(p)].astype(F32) * act
            scaled = grad[0, rb, tile(p)].astype(F32) * gain[:, tile(p)]
            ssd = ((inverse * scaled - gated * pull) * act).astype(BF16)
            ssd_ref[rb, tile(p)] = ssd
            weighted[rb, tile(p)] = (weights[rb, tile(p)] * ssd.astype(F32)).astype(BF16)
    both = mm(split_queries(queries[0], doc[0, 0]), weighted[...], 0, 0)
    visit = both[:state_rows]
    for n, visit_ref in enumerate(visits):

        @pl.when(pl.program_id(0) == n)
        def _(visit_ref=visit_ref):
            visit_ref[...] = visit

    part[...] = both[state_rows:] + share[:1] * visit
    span = state_rows // len(parts)
    for d, piece in enumerate(parts):
        owner = lax.rem(lax.axis_index("dp") + d, len(parts))
        piece[...] = part[pl.ds(pl.multiple_of(owner * span, span), span)]


def back_kernel(
    k, inner_cols, doc, tab_ref, keys, queries, stat_a, stat_b, out, gate, grad, gain, ssd_grad, skip, *rest
):
    base_ref, normed_ref, gate_grad_ref = rest[-3:]
    rows = tab_ref.shape[0]
    doc_start = doc[0, 0]
    halves = head_halves()
    cum_rows = jnp.transpose(tab_ref[...])
    grads = [[ssd_grad[:, tile(p)] * half for half in halves] for p in range(GROUP // 2)]
    for i in range(rows // ROWS):
        rb = row_block(i)
        down = i * ROWS
        scores = mm(keys[0, rb], queries[0, down:], 1, 1)
        s = iota((ROWS, rows - down), 0) + down
        t = iota((ROWS, rows - down), 1) + down
        same = (s <= t) & ((t < doc_start) | (s >= doc_start))
        scores = jnp.where(same, scores, 0.0)
        tab = tab_ref[rb]
        inverse, pull = norm_factors(inner_cols, stat_a[rb] + stat_b[rb])
        for p in range(GROUP // 2):
            wide = ssd_grad[rb, tile(p)].astype(F32)
            total = two_heads(skip[...], k * GROUP + 2 * p) * wide
            for half in range(2):
                h = 2 * p + half
                gap = tab[:, h : h + 1] - cum_rows[h : h + 1, down:]
                mixing = (scores * jnp.exp(jnp.minimum(gap, 0.0))).astype(BF16)
                total += mm(mixing, grads[p][half][down:])
            base_ref[rb, tile(p)] = total
            value = gate[0, rb, tile(p)].astype(F32)
            act, sigmoid = silu(value)
            slope = sigmoid * (1.0 + value * (1.0 - sigmoid))
            wide_out = out[rb, tile(p)].astype(F32)
            gated = wide_out * act
            gains = gain[:, tile(p)]
            scaled = grad[0, rb, tile(p)].astype(F32) * gains
            normed_ref[0, rb, tile(p)] = (gated * inverse * gains).astype(BF16)
            gated_grad = inverse * scaled - gated * pull
            gate_grad_ref[0, rb, tile(p)] = (gated_grad * wide_out * slope).astype(BF16)


def close_kernel(wide, base, adjoint, arrived, keys, *rest):
    grad_ref = rest[-1]
    total = arrived[...] if adjoint is None else adjoint[...] + arrived[...]
    reads = mm(keys[0], total.astype(BF16))
    weights = spread_weights(wide[...], KIND_OUT, base.shape[1])
    grad_ref[0] = (base[...] + weights * reads).astype(BF16)


def add_kernel(*refs):
    refs[-1][...] = sum((r[...] for r in refs[1:-1]), refs[0][...])


def split_add_kernel(parts, *refs):
    total, pieces = refs[-1], refs[-1 - parts : -1]
    span = total.shape[1]
    for n in range(parts):
        rows = slice(n * span, (n + 1) * span)
        total[n] = sum((r[rows] for r in refs[1 : -1 - parts]), refs[0][rows])
    for d, piece in enumerate(pieces):
        piece[...] = total[lax.rem(lax.axis_index("ctx") + d, parts)]


def join_kernel(parts, *refs):
    out, total = refs[-2:]
    span = total.shape[1]
    for d, piece in enumerate(refs[:parts]):
        total[lax.rem(lax.axis_index("ctx") + parts - d, parts)] = piece[...]
    for n in range(parts):
        out[n * span : (n + 1) * span] = total[n]


def derive_kernel(chunks, pieces, prompt_keys, *rest):
    cols, parts = rest[:chunks], rest[chunks : chunks + pieces]
    prompt_ref, start_ref, total = rest[chunks + pieces :]
    span = parts[0].shape[0]
    for d, piece in enumerate(parts):
        owner = lax.rem(lax.axis_index("dp") + pieces - d, pieces)
        total[pl.ds(pl.multiple_of(owner * span, span), span)] = piece[...]
    prompt_rows = prompt_keys.shape[0]
    keys = prompt_keys[...].astype(F32)
    for k in range(chunks):
        width = cols[k].shape[1]
        span = slice(k * width, (k + 1) * width)
        grads = total[:, span]
        start_ref[:, span] = cols[k][prompt_rows : prompt_rows + 1] * grads
        prompt_ref[:, span] = cols[k][:prompt_rows] * mm(keys, grads, precision=EXACT)


def ring(count, distance):
    return [(i, (i + distance) % count) for i in range(count)]


def shape(*dims, dtype=F32):
    return jax.ShapeDtypeStruct(dims, dtype)


def body(
    seq_in,
    gate_in,
    keys_in,
    queries_in,
    step_rate,
    doc_starts,
    skip_gain,
    norm_gain,
    prompt_in,
    prompt_keys,
    prompt_rate,
    start_state,
    out_grad,
):
    _, rows, cols = seq_in.shape
    state_rows = keys_in.shape[2]
    heads = step_rate.shape[2]
    prompt_rows = prompt_in.shape[0]
    chunks = heads // GROUP
    width = cols // chunks
    tensors = lax.axis_size("tensor")
    inner_cols = cols * tensors
    count = lax.axis_size("ctx")
    step = jnp.swapaxes(step_rate, 1, 2)
    skip = skip_gain.reshape(1, heads)
    gain = norm_gain.reshape(1, cols)
    each = range(chunks)
    message = shape(state_rows + EXTRA, width)
    summary = shape(state_rows, width)
    block = shape(rows, width)
    block_low = shape(rows, width, dtype=BF16)
    full = shape(*seq_in.shape, dtype=BF16)
    part_shape = shape(state_rows, cols)

    def blocked(array, k):
        return columns(array, k, width)

    def run(kernel, out, ins, after=(), hold=(), alias=None, scratch=(), limit=16, steps=1):
        held = len(ins) + len(after)
        made = held + len(hold)

        def ordered(*refs):
            kernel(*refs[: len(ins)], *refs[made : made + len(out)], *refs[made + len(out) + len(hold) :])

        extra = [(a, ANYWHERE) for a in (*after, *hold)]
        out = list(out)
        results = out + [(shape(*h.shape, dtype=h.dtype), ANYWHERE) for h in hold]
        return call(
            ordered,
            [whole(s) if spec is None else spec for s, spec in results],
            [whole(a) if spec is None else spec for a, spec in ins + extra],
            [s for s, _ in results],
            alias={**(alias or {}), **{held + i: len(out) + i for i in range(len(hold))}},
            scratch=scratch,
            limit=limit,
            steps=steps,
        )(*[a for a, _ in ins + extra])

    tabs, wides, firsts, moves, lates, sums, throughs, lows, col_tabs = ([] for _ in range(9))
    made = (tabs, wides, firsts, moves, lates, sums, throughs, lows, col_tabs)
    made_shapes = [
        shape(rows, LANES),
        shape(rows, LANES, dtype=BF16),
        message,
        message,
        message,
        message,
        message,
        shape(state_rows, width, dtype=BF16),
        shape(prompt_rows + 24, width),
    ]

    def open_chunks(ks, after):
        ins = [
            (step, False),
            (keys_in, False),
            (seq_in, True),
            (prompt_in, True),
            (prompt_keys, False),
            (prompt_rate, False),
            (start_state, True),
        ]
        cut = [c for _, c in ins]
        blocks = [a.shape[:-1] + (len(ks) * width,) if c else a.shape for a, c in ins]
        out = run(
            functools.partial(open_from_hbm, ks, cut, len(made)),
            [(s, None) for s in made_shapes] * len(ks),
            [(doc_starts, SCALAR)] + [(a, ANYWHERE) for a, _ in ins],
            after=after,
            scratch=[pltpu.VMEM(b, a.dtype) for b, (a, _) in zip(blocks, ins)]
            + [pltpu.SemaphoreType.DMA((len(ins),))],
            limit=PLIM,
        )
        for place, k in enumerate(ks):
            for held, one in zip(made, out[place * len(made) :]):
                held.append(one)
            arrived[k] = edge_up(firsts[k], 0)

    def chain_step(k, arrived, move, mine, after=()):
        return run(
            step_kernel,
            [(shape(*move.shape), None)] * 2,
            [(arrived, None), (move, None), (throughs[k], None)] + [(m, None) for m in mine],
            after=after,
        )

    def edge_up(array, edge):
        return lax.ppermute(array, "ctx", [(edge, edge + 1)])

    def within(k, after, hold):
        base, *held = run(
            functools.partial(within_kernel, k),
            [(block, None)],
            [
                (doc_starts, SCALAR),
                (tabs[k], None),
                (keys_in, None),
                (queries_in, None),
                (seq_in, blocked(seq_in, k)),
                (skip, None),
            ],
            after=after,
            hold=hold,
        )
        bases.append(base)
        return held

    outs, shares, stats, bases = [], [], [], []
    out_shape, share_shape = shape(rows, cols, dtype=BF16), shape(EXTRA, cols)


    def gates(k, hold):
        kernel, held, alias = gate_kernel, [], {}
        if stats:
            held = [(stats[-1], None), (outs[-1], ANYWHERE), (shares[-1], ANYWHERE)]
            alias = {11: 0, 12: 2}
        else:
            kernel = lambda *refs: gate_kernel(*refs[:10], None, *refs[10:])
        out, stat, share, *held = run(
            kernel,
            [
                (out_shape, blocked(out_shape, k)),
                (shape(rows, 8), None),
                (share_shape, blocked(share_shape, k)),
            ],
            [
                (doc_starts, SCALAR),
                (wides[k], None),
                (bases[k], None),
                (sums[k], None),
                (arrived[k], None),
                (lows[k], None),
                (queries_in, None),
                (gate_in, blocked(gate_in, k)),
                (out_grad, blocked(out_grad, k)),
                (gain, blocked(gain, k)),
            ]
            + held,
            alias=alias,
            hold=hold,
        )
        outs.append(out)
        shares.append(share)
        stats.append(stat)
        return held

    last = count - 2
    arrived = [None] * chunks
    open_chunks([0], [])
    pairs = [list(each)[k : k + 2] for k in range(1, chunks, 2)]
    for ks in pairs[:1]:
        open_chunks(ks, [])
    for edge in range(1, max(last, 2)):
        for k in each:
            sent = []
            if edge < last:
                sums[k], *sent = chain_step(k, arrived[k], moves[k], [sums[k]])
                arrived[k] = edge_up(sent[0], edge)
            if edge == 1 and k + 1 < len(pairs):
                open_chunks(pairs[k + 1], sent)
    lag = 2
    for k in range(chunks + lag):
        if k < chunks:
            if k >= lag:
                gates(k - lag, [])
            sent = []
            if last > 0:
                sums[k], *sent = chain_step(k, arrived[k], lates[k], [sums[k]])
                arrived[k] = edge_up(sent[0], last)
            lates[k + 1 : k + 2] = within(k, sent, lates[k + 1 : k + 2])
        else:
            gates(k - lag, [])
    stat = stats[-1]
    other = lax.ppermute(stat, "tensor", ring(tensors, 1))

    def edge_down(array, edge):
        return lax.ppermute(array, "ctx", [(edge, edge - 1)])

    def edge_down(array, edge):
        return lax.ppermute(array, "ctx", [(edge, edge - 1)])

    def moving(array, width):
        lead = (0,) * (array.ndim - 1)
        return pl.BlockSpec(array.shape[:-1] + (width,), lambda s: lead + (s,))

    groups = lax.axis_size("dp")
    piece = shape(state_rows // groups, cols)
    result = run(
        functools.partial(visit_kernel, inner_cols, chunks),
        [(out_shape, moving(out_shape, width))] + [(summary, None)] * chunks + [(piece, moving(piece, width))] * groups,
        [
            (doc_starts, SCALAR),
            (stat, None),
            (other, None),
            (outs[-1], moving(outs[-1], width)),
            (gate_in, moving(gate_in, width)),
            (out_grad, moving(out_grad, width)),
            (gain, moving(gain, width)),
            (queries_in, None),
            (shares[-1], moving(shares[-1], width)),
        ]
        + [(w, None) for w in wides],
        scratch=[pltpu.VMEM((rows, width), BF16), pltpu.VMEM((state_rows, width), F32)],
        steps=chunks,
        limit=VLIM,
    )
    ssd_grad, visits, parts = result[0], result[1 : 1 + chunks], result[1 + chunks :]
    for k in each:
        arrived[k] = edge_down(visits[k], count - 1)

    back_bases = []
    normed = gate_grad = None

    def back(k, after, hold):
        ins = [
            (doc_starts, SCALAR),
            (tabs[k], None),
            (keys_in, None),
            (queries_in, None),
            (stat, None),
            (other, None),
            (outs[-1], blocked(outs[-1], k)),
            (gate_in, blocked(gate_in, k)),
            (out_grad, blocked(out_grad, k)),
            (gain, blocked(gain, k)),
            (ssd_grad, blocked(ssd_grad, k)),
            (skip, None),
        ]
        alias = {}
        if normed is not None:
            alias = {len(ins): 1, len(ins) + 1: 2}
            ins += [(normed, ANYWHERE), (gate_grad, ANYWHERE)]
        base, *results = run(
            functools.partial(back_kernel, k, inner_cols),
            [(block, None), (full, blocked(full, k)), (full, blocked(full, k))],
            ins,
            after=after,
            hold=hold,
            alias=alias,
        )
        back_bases.append(base)
        return results

    normed, gate_grad, *parts = back(0, [], list(parts))
    from_groups = [lax.ppermute(parts[d], "dp", ring(groups, d)) for d in range(1, groups)]
    adjoints = [None] * chunks
    sent = []
    for edge in range(count - 2, 0, -1):
        for k in each:
            held = [] if adjoints[k] is None else [adjoints[k]]
            order = back_bases[-1:] if edge == 1 else []
            adjoints[k], message_out = chain_step(k, arrived[k], visits[k], held, order)
            sent = [message_out]
            arrived[k] = edge_down(message_out, edge)
            if edge == 1 and 0 < k < chunks - 1:
                normed, gate_grad = back(k, sent + [arrived[k - 1]], [])
    for k in range(len(back_bases), chunks - 1):
        normed, gate_grad = back(k, [], [])

    small = shape(piece.shape[0] // count, cols)
    mine = run(
        functools.partial(split_add_kernel, count),
        [(small, None)] * count,
        [(p, None) for p in (parts[0], *from_groups)],
        after=sent + back_bases[-1:] + arrived[-2:-1],
        scratch=[pltpu.VMEM((count,) + small.shape, F32)],
    )
    from_blocks = [lax.ppermute(mine[d], "ctx", ring(count, d)) for d in range(1, count)]
    normed, gate_grad = back(chunks - 1, [mine[0], arrived[-1]], [])
    (own,) = run(add_kernel, [(small, None)], [(p, None) for p in (mine[0], *from_blocks)], after=back_bases[-1:])
    owned = [own] + [lax.ppermute(own, "ctx", ring(count, d)) for d in range(1, count)]
    (total,) = run(
        functools.partial(join_kernel, count),
        [(piece, None)],
        [(p, None) for p in owned],
        scratch=[pltpu.VMEM((count,) + small.shape, F32)],
    )
    totals = [total] + [lax.ppermute(total, "dp", ring(groups, d)) for d in range(1, groups)]

    grad_in = None
    for k in each:
        ins = [(wides[k], None), (back_bases[k], None)]
        kernel = close_kernel
        if adjoints[k] is None:
            kernel = lambda wide, base, *refs: close_kernel(wide, base, None, *refs)
        else:
            ins.append((adjoints[k], None))
        ins += [(arrived[k], None), (keys_in, None)]
        alias = {}
        if grad_in is not None:
            alias = {len(ins): 0}
            ins.append((grad_in, ANYWHERE))
        (grad_in,) = run(kernel, [(full, blocked(full, k))], ins, alias=alias)

    grad_prompt, grad_start = run(
        functools.partial(derive_kernel, chunks, groups),
        [(shape(prompt_rows, cols), None), (part_shape, None)],
        [(a, None) for a in (prompt_keys, *col_tabs, *totals)],
        after=[grad_in],
        scratch=[pltpu.VMEM((state_rows, cols), F32)],
    )
    return normed, grad_in, gate_grad, grad_prompt, grad_start


def solution(mesh):
    return jax.shard_map(
        body,
        mesh=mesh,
        in_specs=(
            P("dp", "ctx", "tensor"),
            P("dp", "ctx", "tensor"),
            P("dp", "ctx", None),
            P("dp", "ctx", None),
            P("dp", "ctx", "tensor"),
            P("dp", "ctx"),
            P("tensor"),
            P("tensor"),
            P(None, "tensor"),
            P(),
            P(None, "tensor"),
            P(None, "tensor"),
            P("dp", "ctx", "tensor"),
        ),
        out_specs=(
            P("dp", "ctx", "tensor"),
            P("dp", "ctx", "tensor"),
            P("dp", "ctx", "tensor"),
            P(None, "tensor"),
            P(None, "tensor"),
        ),
        check_vma=False,
    )
```

```python
import functools

import jax
import jax.numpy as jnp
from jax import lax
from jax.experimental import pallas as pl
from jax.experimental.pallas import tpu as pltpu
from jax.sharding import PartitionSpec as P

HEAD_DIM = 64
EPSILON = 1e-05
LANES = 128
VLIM = 32
BETWEEN = 4
WAITED = 3
LATE = 4
PLIM = 24
GROUP = 8
KIND_IN, KIND_OUT = 1, 3
EXTRA = 8
ROWS = 128

F32 = jnp.float32
BF16 = jnp.bfloat16
EXACT = lax.Precision.HIGHEST


def iota(shape, dim):
    return lax.broadcasted_iota(jnp.int32, shape, dim)


def mm(a, b, da=1, db=0, precision=None):
    return lax.dot_general(
        a, b, (((da,), (db,)), ((), ())), precision=precision, preferred_element_type=F32
    )


def two_heads(table, first):
    rows = table.shape[0]
    left = jnp.broadcast_to(table[:, first : first + 1], (rows, LANES))
    right = jnp.broadcast_to(table[:, first + 1 : first + 2], (rows, LANES))
    return jnp.where(iota((rows, LANES), 1) < HEAD_DIM, left, right)


def spread_weights(wide, kind, width):
    lane, col = iota((LANES, width), 0), iota((LANES, width), 1)
    part = lane // GROUP
    hit = ((part == kind) | (part == kind + 1)) & ((lane & (GROUP - 1)) == col // HEAD_DIM)
    return mm(wide, jnp.where(hit, 1.0, 0.0).astype(BF16))


def split_queries(queries, doc_start):
    rows, width = queries.shape
    ahead = iota((rows, width), 0) < doc_start
    wide = queries.astype(F32)
    both = [jnp.where(ahead, wide, 0.0), jnp.where(ahead, 0.0, wide)]
    return jnp.concatenate(both, axis=1).astype(BF16)


def tile(p):
    return slice(p * LANES, (p + 1) * LANES)


def row_block(i):
    return slice(i * ROWS, (i + 1) * ROWS)


def each_pair(one):
    def step(p, carry):
        one(p, pl.ds(pl.multiple_of(p * LANES, LANES), LANES))
        return carry

    lax.fori_loop(0, GROUP // 2, step, 0)


def each_block(rows, one):
    def step(i, carry):
        one(pl.ds(pl.multiple_of(i * ROWS, ROWS), ROWS))
        return carry

    lax.fori_loop(0, rows // ROWS, step, 0)


def turn(table, p):
    return pltpu.roll(table, lax.rem(LANES - 2 * p, LANES), 1)


def call(kernel, outs, ins, out_shapes, scratch=(), alias=None, limit=16, steps=1):
    return pl.pallas_call(
        kernel,
        grid=(steps,),
        in_specs=ins,
        out_specs=outs,
        out_shape=out_shapes,
        scratch_shapes=list(scratch),
        input_output_aliases=alias or {},
        cost_estimate=pl.CostEstimate(flops=0, bytes_accessed=0, transcendentals=0),
        compiler_params=pltpu.CompilerParams(vmem_limit_bytes=limit * 2**20),
    )


def whole(array):
    zeros = (0,) * array.ndim
    return pl.BlockSpec(array.shape, lambda s: zeros)


def columns(array, k, width):
    lead = (0,) * (array.ndim - 1)
    return pl.BlockSpec(array.shape[:-1] + (width,), lambda s: lead + (k,))


SCALAR = pl.BlockSpec(memory_space=pltpu.SMEM)
ANYWHERE = pl.BlockSpec(memory_space=pl.ANY)


def silu(value):
    sigmoid = 0.5 + 0.5 * jnp.tanh(0.5 * value)
    return value * sigmoid, sigmoid


def open_kernel(
    k, doc, step_ref, keys, seq, prompt_in, prompt_keys, rate, state,
    tab_ref, wide_ref, first_ref, move_ref, late_ref, mine_ref, through_ref, low_ref, cols_ref,
):
    heads, rows = step_ref.shape[1:]
    doc_start = doc[0, 0]
    step = step_ref[0]
    hh, ll = iota((heads, LANES), 0), iota((heads, LANES), 1)
    spread = jnp.where((ll < 5 * GROUP) & (hh == k * GROUP + (ll & (GROUP - 1))), 1.0, 0.0)
    spread = spread.astype(BF16)
    tri = jnp.where(iota((rows, rows), 0) >= iota((rows, rows), 1), 1.0, 0.0).astype(BF16)
    high = step.astype(BF16)
    rest = step - high.astype(F32)
    middle = rest.astype(BF16)
    low = (rest - middle.astype(F32)).astype(BF16)
    step_rep = jnp.zeros((rows, LANES), F32)
    cum = jnp.zeros((rows, LANES), F32)
    for part in (low, middle, high):
        rep = mm(part, spread, 0, 0)
        step_rep = step_rep + rep
        cum = cum + mm(tri, rep.astype(BF16))
    before = cum - step_rep
    pos = iota((rows, LANES), 0)
    kind = iota((rows, LANES), 1) // GROUP
    has = doc_start < rows
    ex_start = jnp.sum(jnp.where(pos == doc_start, before, 0.0), axis=0, keepdims=True)
    end = cum[rows - 1 : rows]
    tail_start = jnp.where(has, doc_start, 0)
    arg = jnp.where(kind < KIND_OUT, jnp.where(pos < doc_start, 0.0, ex_start) - cum, cum - end)
    keep = (kind < KIND_OUT) | (pos >= tail_start)
    weights = jnp.where(keep, jnp.exp(jnp.minimum(arg, 0.0)), 0.0)
    tab_ref[...] = cum
    head_part = weights.astype(BF16).astype(F32)
    is_head = (kind == KIND_IN) | (kind == KIND_OUT)
    wide = jnp.where(is_head, head_part, weights - head_part).astype(BF16)
    wide_ref[...] = wide
    through = jnp.where(has, 0.0, jnp.exp(-end))
    leave = jnp.where(has, jnp.exp(ex_start - end), 0.0)

    prompt_rows = rate.shape[0]
    square = (prompt_rows, prompt_rows)
    later = jnp.where(iota(square, 0) < iota(square, 1), 1.0, 0.0)
    spread_weight = jnp.exp(-mm(later, rate[...], precision=EXACT))
    carry = jnp.exp(-jnp.sum(rate[...], axis=0, keepdims=True))
    for p in range(GROUP // 2):
        cols_ref[:prompt_rows, tile(p)] = two_heads(spread_weight, k * GROUP + 2 * p)
        for place, row in ((0, two_heads(carry, k * GROUP + 2 * p)), (8, two_heads(through, 2 * p))):
            rows_here = slice(prompt_rows + place, prompt_rows + place + 8)
            cols_ref[rows_here, tile(p)] = jnp.broadcast_to(row, (8, LANES))
        cols_ref[prompt_rows + 16 : prompt_rows + 24, tile(p)] = jnp.broadcast_to(
            two_heads(leave, 2 * p), (8, LANES)
        )
    state_rows, width = state.shape
    weighted = (seq[0].astype(F32) * spread_weights(wide, KIND_OUT, width)).astype(BF16)
    field = mm(
        prompt_keys[...].astype(F32), cols_ref[:prompt_rows] * prompt_in[...].astype(F32), 0, 0, EXACT
    )
    start = field + cols_ref[prompt_rows : prompt_rows + 1] * state[...]
    through_cols = cols_ref[prompt_rows + 8 : prompt_rows + 9]
    through_ref[...] = jnp.broadcast_to(through_cols, through_ref.shape)
    leave_cols = cols_ref[prompt_rows + 16 : prompt_rows + 17]
    move = mm(keys[0], weighted, 0, 0) + leave_cols * start
    is_first = lax.axis_index("ctx") == 0
    low_ref[...] = start.astype(BF16)
    mine_ref[:state_rows] = jnp.where(is_first, start, 0.0)
    move_ref[:state_rows] = move
    late_ref[:state_rows] = move
    first_ref[:state_rows] = through_cols * start + move
    ones = jnp.ones((EXTRA, width), F32)
    mine_ref[state_rows:] = jnp.where(is_first, ones, 0.0)
    extra = jnp.broadcast_to(leave_cols, (EXTRA, width))
    move_ref[state_rows:] = extra
    late_ref[state_rows:] = extra
    first_ref[state_rows:] = through_cols + extra


def open_from_hbm(ks, cut, outs, doc, *refs):
    ins = len(cut)
    held, buffers, sems = refs[:ins], refs[-1 - ins : -1], refs[-1]
    made = refs[-1 - ins - outs * len(ks) : -1 - ins]
    copies = []
    for n, (source, buffer) in enumerate(zip(held, buffers)):
        width = buffer.shape[-1]
        columns_here = pl.ds(ks[0] * (width // len(ks)) if cut[n] else 0, width)
        lead = (slice(None),) * (len(buffer.shape) - 1)
        copies.append(pltpu.make_async_copy(source.at[lead + (columns_here,)], buffer, sems.at[n]))
    for copy in copies:
        copy.start()
    for copy in copies:
        copy.wait()
    for place, k in enumerate(ks):
        mine = []
        for buffer, is_cut in zip(buffers, cut):
            width = buffer.shape[-1] // len(ks)
            lead = (slice(None),) * (len(buffer.shape) - 1)
            mine.append(buffer.at[lead + (pl.ds(place * width, width),)] if is_cut else buffer)
        open_kernel(k, doc, *mine, *made[place * outs : (place + 1) * outs])


def step_kernel(arrived, move, through, *rest):
    mine, (sum_ref, send_ref) = rest[:-2], rest[-2:]
    total = arrived[...] if not mine else mine[0][...] + arrived[...]
    sum_ref[...] = total
    send_ref[...] = through[: total.shape[0]] * total + move[...]


def head_halves():
    lane = iota((1, LANES), 1)
    return [jnp.where(half, 1.0, 0.0).astype(BF16) for half in (lane < HEAD_DIM, lane >= HEAD_DIM)]


def within_kernel(k, doc, tab_ref, keys, queries, seq, skip, base_ref, cum_rows, scores, skips):
    rows = tab_ref.shape[0]
    doc_start = doc[0, 0]
    halves = head_halves()
    turned_sums = jnp.transpose(tab_ref[...])
    for h in range(GROUP):
        cum_rows[h] = jnp.broadcast_to(turned_sums[h : h + 1], cum_rows.shape[1:])
    for p in range(GROUP // 2):
        skips[:, tile(p)] = jnp.broadcast_to(two_heads(skip[...], k * GROUP + 2 * p), (8, LANES))
    for i in range(rows // ROWS):
        upto = (i + 1) * ROWS
        t = iota((ROWS, upto), 0) + i * ROWS
        s = iota((ROWS, upto), 1)
        same = (s <= t) & ((t < doc_start) | (s >= doc_start))
        scores[row_block(i), :upto] = jnp.where(same, mm(queries[0, row_block(i)], keys[0, :upto], 1, 1), 0.0)

    def pair(p, here):
        turned = turn(tab_ref[...], p)
        values = [seq[0, :, here] * half for half in halves]
        for i in range(rows // ROWS):
            upto = (i + 1) * ROWS
            total = skips[:1, here] * seq[0, row_block(i), here].astype(F32)
            for half in range(2):
                gap = cum_rows[2 * p + half, :1, :upto] - turned[row_block(i), half : half + 1]
                mixing = (scores[row_block(i), :upto] * jnp.exp(jnp.minimum(gap, 0.0))).astype(BF16)
                total += mm(mixing, values[half][:upto])
            base_ref[row_block(i), here] = total

    each_pair(pair)


def gate_kernel(
    doc, wide, base, mine, arrived, low, queries, gate, grad, gain, before, *rest
):
    out_ref, stat_ref, share_ref = rest[-3:]
    rows, width = base.shape
    state_rows = low.shape[0]
    state_in = mine[...] + arrived[...]
    share_ref[...] = state_in[state_rows:]
    fields = jnp.concatenate([state_in[:state_rows].astype(BF16), low[...]], axis=0)
    reads = mm(split_queries(queries[0], doc[0, 0]), fields)
    weights = spread_weights(wide[...], KIND_IN, width)
    for i in range(rows // ROWS):
        rb = row_block(i)
        squares = jnp.zeros((ROWS, LANES), F32)
        inner = jnp.zeros((ROWS, LANES), F32)
        for p in range(GROUP // 2):
            out = (base[rb, tile(p)] + weights[rb, tile(p)] * reads[rb, tile(p)]).astype(BF16)
            out_ref[rb, tile(p)] = out
            act, _ = silu(gate[0, rb, tile(p)].astype(F32))
            gated = out.astype(F32) * act
            squares += gated * gated
            inner += grad[0, rb, tile(p)].astype(F32) * gain[:, tile(p)] * gated
        lane = iota((ROWS, 8), 1)
        sums = jnp.where(
            lane == 0,
            jnp.sum(squares, axis=1, keepdims=True),
            jnp.where(lane == 1, jnp.sum(inner, axis=1, keepdims=True), 0.0),
        )
        stat_ref[rb] = sums if before is None else before[rb] + sums


def norm_factors(inner_cols, stat):
    inverse = lax.rsqrt(stat[:, 0:1] / inner_cols + EPSILON)
    pull = stat[:, 1:2] * inverse * inverse * inverse / inner_cols
    shape = (stat.shape[0], LANES)
    return jnp.broadcast_to(inverse, shape), jnp.broadcast_to(pull, shape)


def visit_kernel(
    inner_cols, chunks, doc, stat_a, stat_b, out, gate, grad, gain, queries, share, *rest
):
    wides, ssd_ref, weighted, part = rest[:chunks], rest[chunks], rest[-2], rest[-1]
    visits, parts = rest[chunks + 1 : 2 * chunks + 1], rest[2 * chunks + 1 : -2]
    wide = wides[0][...]
    for n in range(1, chunks):
        wide = jnp.where(pl.program_id(0) == n, wides[n][...], wide)
    rows, width = out.shape
    state_rows = queries.shape[2]
    weights = spread_weights(wide, KIND_IN, width)
    for i in range(rows // ROWS):
        rb = row_block(i)
        inverse, pull = norm_factors(inner_cols, stat_a[rb] + stat_b[rb])
        for p in range(GROUP // 2):
            act, _ = silu(gate[0, rb, tile(p)].astype(F32))
            gated = out[rb, tile(p)].astype(F32) * act
            scaled = grad[0, rb, tile(p)].astype(F32) * gain[:, tile(p)]
            ssd = ((inverse * scaled - gated * pull) * act).astype(BF16)
            ssd_ref[rb, tile(p)] = ssd
            weighted[rb, tile(p)] = (weights[rb, tile(p)] * ssd.astype(F32)).astype(BF16)
    both = mm(split_queries(queries[0], doc[0, 0]), weighted[...], 0, 0)
    visit = both[:state_rows]
    for n, visit_ref in enumerate(visits):

        @pl.when(pl.program_id(0) == n)
        def _(visit_ref=visit_ref):
            visit_ref[...] = visit

    part[...] = both[state_rows:] + share[:1] * visit
    span = state_rows // len(parts)
    for d, piece in enumerate(parts):
        owner = lax.rem(lax.axis_index("dp") + d, len(parts))
        piece[...] = part[pl.ds(pl.multiple_of(owner * span, span), span)]


def back_kernel(
    k, inner_cols, doc, tab_ref, keys, queries, stat_a, stat_b, out, gate, grad, gain, ssd_grad, skip, *rest
):
    base_ref, normed_ref, gate_grad_ref, cum_rows, scores, skips = rest[-6:]
    rows = tab_ref.shape[0]
    doc_start = doc[0, 0]
    halves = head_halves()
    turned_sums = jnp.transpose(tab_ref[...])
    for h in range(GROUP):
        cum_rows[h] = jnp.broadcast_to(turned_sums[h : h + 1], cum_rows.shape[1:])
    for p in range(GROUP // 2):
        skips[:, tile(p)] = jnp.broadcast_to(two_heads(skip[...], k * GROUP + 2 * p), (8, LANES))
    for i in range(rows // ROWS):
        down = i * ROWS
        s = iota((ROWS, rows - down), 0) + down
        t = iota((ROWS, rows - down), 1) + down
        same = (s <= t) & ((t < doc_start) | (s >= doc_start))
        scores[row_block(i), down:] = jnp.where(same, mm(keys[0, row_block(i)], queries[0, down:], 1, 1), 0.0)

    def pair(p, here):
        turned = turn(tab_ref[...], p)
        grads = [ssd_grad[:, here] * half for half in halves]
        for i in range(rows // ROWS):
            down = i * ROWS
            total = skips[:1, here] * ssd_grad[row_block(i), here].astype(F32)
            for half in range(2):
                gap = turned[row_block(i), half : half + 1] - cum_rows[2 * p + half, :1, down:]
                mixing = (scores[row_block(i), down:] * jnp.exp(jnp.minimum(gap, 0.0))).astype(BF16)
                total += mm(mixing, grads[half][down:])
            base_ref[row_block(i), here] = total

    each_pair(pair)

    def one(rb):
        inverse, pull = norm_factors(inner_cols, stat_a[rb] + stat_b[rb])
        for p in range(GROUP // 2):
            value = gate[0, rb, tile(p)].astype(F32)
            act, sigmoid = silu(value)
            slope = sigmoid * (1.0 + value * (1.0 - sigmoid))
            wide_out = out[rb, tile(p)].astype(F32)
            gated = wide_out * act
            gains = gain[:, tile(p)]
            scaled = grad[0, rb, tile(p)].astype(F32) * gains
            normed_ref[0, rb, tile(p)] = (gated * inverse * gains).astype(BF16)
            gated_grad = inverse * scaled - gated * pull
            gate_grad_ref[0, rb, tile(p)] = (gated_grad * wide_out * slope).astype(BF16)

    each_block(rows, one)


def close_kernel(wide, base, adjoint, arrived, keys, *rest):
    grad_ref = rest[-1]
    total = arrived[...] if adjoint is None else adjoint[...] + arrived[...]
    reads = mm(keys[0], total.astype(BF16))
    weights = spread_weights(wide[...], KIND_OUT, base.shape[1])
    grad_ref[0] = (base[...] + weights * reads).astype(BF16)


def add_kernel(*refs):
    refs[-1][...] = sum((r[...] for r in refs[1:-1]), refs[0][...])


def split_add_kernel(parts, *refs):
    total, pieces = refs[-1], refs[-1 - parts : -1]
    span = total.shape[1]
    for n in range(parts):
        rows = slice(n * span, (n + 1) * span)
        total[n] = sum((r[rows] for r in refs[1 : -1 - parts]), refs[0][rows])
    for d, piece in enumerate(pieces):
        piece[...] = total[lax.rem(lax.axis_index("ctx") + d, parts)]


def join_kernel(parts, *refs):
    out, total = refs[-2:]
    span = total.shape[1]
    for d, piece in enumerate(refs[:parts]):
        total[lax.rem(lax.axis_index("ctx") + parts - d, parts)] = piece[...]
    for n in range(parts):
        out[n * span : (n + 1) * span] = total[n]


def derive_kernel(chunks, pieces, prompt_keys, *rest):
    cols, parts = rest[:chunks], rest[chunks : chunks + pieces]
    prompt_ref, start_ref, total = rest[chunks + pieces :]
    span = parts[0].shape[0]
    for d, piece in enumerate(parts):
        owner = lax.rem(lax.axis_index("dp") + pieces - d, pieces)
        total[pl.ds(pl.multiple_of(owner * span, span), span)] = piece[...]
    prompt_rows = prompt_keys.shape[0]
    keys = prompt_keys[...].astype(F32)
    for k in range(chunks):
        width = cols[k].shape[1]
        span = slice(k * width, (k + 1) * width)
        grads = total[:, span]
        start_ref[:, span] = cols[k][prompt_rows : prompt_rows + 1] * grads
        prompt_ref[:, span] = cols[k][:prompt_rows] * mm(keys, grads, precision=EXACT)


def ring(count, distance):
    return [(i, (i + distance) % count) for i in range(count)]


def shape(*dims, dtype=F32):
    return jax.ShapeDtypeStruct(dims, dtype)


def body(
    seq_in,
    gate_in,
    keys_in,
    queries_in,
    step_rate,
    doc_starts,
    skip_gain,
    norm_gain,
    prompt_in,
    prompt_keys,
    prompt_rate,
    start_state,
    out_grad,
):
    _, rows, cols = seq_in.shape
    state_rows = keys_in.shape[2]
    heads = step_rate.shape[2]
    prompt_rows = prompt_in.shape[0]
    chunks = heads // GROUP
    width = cols // chunks
    tensors = lax.axis_size("tensor")
    inner_cols = cols * tensors
    count = lax.axis_size("ctx")
    step = jnp.swapaxes(step_rate, 1, 2)
    skip = skip_gain.reshape(1, heads)
    gain = norm_gain.reshape(1, cols)
    each = range(chunks)
    message = shape(state_rows + EXTRA, width)
    summary = shape(state_rows, width)
    block = shape(rows, width)
    block_low = shape(rows, width, dtype=BF16)
    full = shape(*seq_in.shape, dtype=BF16)
    part_shape = shape(state_rows, cols)

    def blocked(array, k):
        return columns(array, k, width)

    def run(kernel, out, ins, after=(), hold=(), alias=None, scratch=(), limit=16, steps=1):
        held = len(ins) + len(after)
        made = held + len(hold)

        def ordered(*refs):
            kernel(*refs[: len(ins)], *refs[made : made + len(out)], *refs[made + len(out) + len(hold) :])

        extra = [(a, ANYWHERE) for a in (*after, *hold)]
        out = list(out)
        results = out + [(shape(*h.shape, dtype=h.dtype), ANYWHERE) for h in hold]
        return call(
            ordered,
            [whole(s) if spec is None else spec for s, spec in results],
            [whole(a) if spec is None else spec for a, spec in ins + extra],
            [s for s, _ in results],
            alias={**(alias or {}), **{held + i: len(out) + i for i in range(len(hold))}},
            scratch=scratch,
            limit=limit,
            steps=steps,
        )(*[a for a, _ in ins + extra])

    tabs, wides, firsts, moves, lates, sums, throughs, lows, col_tabs = ([] for _ in range(9))
    made = (tabs, wides, firsts, moves, lates, sums, throughs, lows, col_tabs)
    made_shapes = [
        shape(rows, LANES),
        shape(rows, LANES, dtype=BF16),
        message,
        message,
        message,
        message,
        message,
        shape(state_rows, width, dtype=BF16),
        shape(prompt_rows + 24, width),
    ]

    def open_chunks(ks, after):
        ins = [
            (step, False),
            (keys_in, False),
            (seq_in, True),
            (prompt_in, True),
            (prompt_keys, False),
            (prompt_rate, False),
            (start_state, True),
        ]
        cut = [c for _, c in ins]
        blocks = [a.shape[:-1] + (len(ks) * width,) if c else a.shape for a, c in ins]
        out = run(
            functools.partial(open_from_hbm, ks, cut, len(made)),
            [(s, None) for s in made_shapes] * len(ks),
            [(doc_starts, SCALAR)] + [(a, ANYWHERE) for a, _ in ins],
            after=after,
            scratch=[pltpu.VMEM(b, a.dtype) for b, (a, _) in zip(blocks, ins)]
            + [pltpu.SemaphoreType.DMA((len(ins),))],
            limit=PLIM,
        )
        for place, k in enumerate(ks):
            for held, one in zip(made, out[place * len(made) :]):
                held.append(one)
            arrived[k] = edge_up(firsts[k], 0)

    def chain_step(k, arrived, move, mine, after=()):
        return run(
            step_kernel,
            [(shape(*move.shape), None)] * 2,
            [(arrived, None), (move, None), (throughs[k], None)] + [(m, None) for m in mine],
            after=after,
        )

    def edge_up(array, edge):
        return lax.ppermute(array, "ctx", [(edge, edge + 1)])

    mixing_scratch = [pltpu.VMEM(s, F32) for s in ((GROUP, 8, rows), (rows, rows), (8, width))]

    def within(k, after, hold):
        base, *held = run(
            functools.partial(within_kernel, k),
            [(block, None)],
            [
                (doc_starts, SCALAR),
                (tabs[k], None),
                (keys_in, None),
                (queries_in, None),
                (seq_in, blocked(seq_in, k)),
                (skip, None),
            ],
            after=after,
            hold=hold,
            scratch=mixing_scratch,
        )
        bases.append(base)
        return held

    outs, shares, stats, bases = [], [], [], []
    out_shape, share_shape = shape(rows, cols, dtype=BF16), shape(EXTRA, cols)


    def gates(k, hold):
        kernel, held, alias = gate_kernel, [], {}
        if stats:
            held = [(stats[-1], None), (outs[-1], ANYWHERE), (shares[-1], ANYWHERE)]
            alias = {11: 0, 12: 2}
        else:
            kernel = lambda *refs: gate_kernel(*refs[:10], None, *refs[10:])
        out, stat, share, *held = run(
            kernel,
            [
                (out_shape, blocked(out_shape, k)),
                (shape(rows, 8), None),
                (share_shape, blocked(share_shape, k)),
            ],
            [
                (doc_starts, SCALAR),
                (wides[k], None),
                (bases[k], None),
                (sums[k], None),
                (arrived[k], None),
                (lows[k], None),
                (queries_in, None),
                (gate_in, blocked(gate_in, k)),
                (out_grad, blocked(out_grad, k)),
                (gain, blocked(gain, k)),
            ]
            + held,
            alias=alias,
            hold=hold,
        )
        outs.append(out)
        shares.append(share)
        stats.append(stat)
        return held

    last = count - 2
    arrived = [None] * chunks
    open_chunks([0], [])
    pairs = [list(each)[k : k + 2] for k in range(1, chunks, 2)]
    for ks in pairs[:1]:
        open_chunks(ks, [])
    for edge in range(1, max(last, 2)):
        for k in each:
            sent = []
            if edge < last:
                sums[k], *sent = chain_step(k, arrived[k], moves[k], [sums[k]])
                arrived[k] = edge_up(sent[0], edge)
            if edge == 1 and k + 1 < len(pairs):
                open_chunks(pairs[k + 1], sent)
    lag = 2
    for k in range(chunks + lag):
        if k < chunks:
            if k >= lag:
                gates(k - lag, [])
            sent = []
            if last > 0:
                sums[k], *sent = chain_step(k, arrived[k], lates[k], [sums[k]])
                arrived[k] = edge_up(sent[0], last)
            lates[k + 1 : k + 2] = within(k, sent, lates[k + 1 : k + 2])
        else:
            gates(k - lag, [])
    stat = stats[-1]
    other = lax.ppermute(stat, "tensor", ring(tensors, 1))

    def edge_down(array, edge):
        return lax.ppermute(array, "ctx", [(edge, edge - 1)])

    def edge_down(array, edge):
        return lax.ppermute(array, "ctx", [(edge, edge - 1)])

    def moving(array, width):
        lead = (0,) * (array.ndim - 1)
        return pl.BlockSpec(array.shape[:-1] + (width,), lambda s: lead + (s,))

    groups = lax.axis_size("dp")
    piece = shape(state_rows // groups, cols)
    result = run(
        functools.partial(visit_kernel, inner_cols, chunks),
        [(out_shape, moving(out_shape, width))] + [(summary, None)] * chunks + [(piece, moving(piece, width))] * groups,
        [
            (doc_starts, SCALAR),
            (stat, None),
            (other, None),
            (outs[-1], moving(outs[-1], width)),
            (gate_in, moving(gate_in, width)),
            (out_grad, moving(out_grad, width)),
            (gain, moving(gain, width)),
            (queries_in, None),
            (shares[-1], moving(shares[-1], width)),
        ]
        + [(w, None) for w in wides],
        scratch=[pltpu.VMEM((rows, width), BF16), pltpu.VMEM((state_rows, width), F32)],
        steps=chunks,
        limit=VLIM,
    )
    ssd_grad, visits, parts = result[0], result[1 : 1 + chunks], result[1 + chunks :]
    for k in each:
        arrived[k] = edge_down(visits[k], count - 1)

    back_bases = []
    normed = gate_grad = None

    def back(k, after, hold):
        ins = [
            (doc_starts, SCALAR),
            (tabs[k], None),
            (keys_in, None),
            (queries_in, None),
            (stat, None),
            (other, None),
            (outs[-1], blocked(outs[-1], k)),
            (gate_in, blocked(gate_in, k)),
            (out_grad, blocked(out_grad, k)),
            (gain, blocked(gain, k)),
            (ssd_grad, blocked(ssd_grad, k)),
            (skip, None),
        ]
        alias = {}
        if normed is not None:
            alias = {len(ins): 1, len(ins) + 1: 2}
            ins += [(normed, ANYWHERE), (gate_grad, ANYWHERE)]
        base, *results = run(
            functools.partial(back_kernel, k, inner_cols),
            [(block, None), (full, blocked(full, k)), (full, blocked(full, k))],
            ins,
            after=after,
            hold=hold,
            alias=alias,
            scratch=mixing_scratch,
        )
        back_bases.append(base)
        return results

    normed, gate_grad, *parts = back(0, [], list(parts))
    from_groups = [lax.ppermute(parts[d], "dp", ring(groups, d)) for d in range(1, groups)]
    adjoints = [None] * chunks
    sent = []
    for edge in range(count - 2, 0, -1):
        for k in each:
            held = [] if adjoints[k] is None else [adjoints[k]]
            order = back_bases[-1:] if edge == 1 else []
            adjoints[k], message_out = chain_step(k, arrived[k], visits[k], held, order)
            sent = [message_out]
            arrived[k] = edge_down(message_out, edge)
            if edge == 1 and 0 < k < BETWEEN:
                normed, gate_grad = back(k, sent + [arrived[k - 1]], [])

    small = shape(piece.shape[0] // count, cols)
    mine = run(
        functools.partial(split_add_kernel, count),
        [(small, None)] * count,
        [(p, None) for p in (parts[0], *from_groups)],
        after=sent + back_bases[-1:] + arrived[WAITED : WAITED + 1],
        scratch=[pltpu.VMEM((count,) + small.shape, F32)],
    )
    from_blocks = [lax.ppermute(mine[d], "ctx", ring(count, d)) for d in range(1, count)]
    for k in range(len(back_bases), LATE):
        normed, gate_grad = back(k, [mine[0], arrived[k]], [])
    (own,) = run(add_kernel, [(small, None)], [(p, None) for p in (mine[0], *from_blocks)], after=back_bases[-1:])
    owned = [own] + [lax.ppermute(own, "ctx", ring(count, d)) for d in range(1, count)]
    for k in range(LATE, chunks):
        normed, gate_grad = back(k, [own, arrived[k]], [])
    (total,) = run(
        functools.partial(join_kernel, count),
        [(piece, None)],
        [(p, None) for p in owned],
        after=back_bases[-1:],
        scratch=[pltpu.VMEM((count,) + small.shape, F32)],
    )
    totals = [total] + [lax.ppermute(total, "dp", ring(groups, d)) for d in range(1, groups)]

    grad_in = None
    for k in each:
        ins = [(wides[k], None), (back_bases[k], None)]
        kernel = close_kernel
        if adjoints[k] is None:
            kernel = lambda wide, base, *refs: close_kernel(wide, base, None, *refs)
        else:
            ins.append((adjoints[k], None))
        ins += [(arrived[k], None), (keys_in, None)]
        alias = {}
        if grad_in is not None:
            alias = {len(ins): 0}
            ins.append((grad_in, ANYWHERE))
        (grad_in,) = run(kernel, [(full, blocked(full, k))], ins, alias=alias)

    grad_prompt, grad_start = run(
        functools.partial(derive_kernel, chunks, groups),
        [(shape(prompt_rows, cols), None), (part_shape, None)],
        [(a, None) for a in (prompt_keys, *col_tabs, *totals)],
        scratch=[pltpu.VMEM((state_rows, cols), F32)],
    )
    return normed, grad_in, gate_grad, grad_prompt, grad_start


def solution(mesh):
    return jax.shard_map(
        body,
        mesh=mesh,
        in_specs=(
            P("dp", "ctx", "tensor"),
            P("dp", "ctx", "tensor"),
            P("dp", "ctx", None),
            P("dp", "ctx", None),
            P("dp", "ctx", "tensor"),
            P("dp", "ctx"),
            P("tensor"),
            P("tensor"),
            P(None, "tensor"),
            P(),
            P(None, "tensor"),
            P(None, "tensor"),
            P("dp", "ctx", "tensor"),
        ),
        out_specs=(
            P("dp", "ctx", "tensor"),
            P("dp", "ctx", "tensor"),
            P("dp", "ctx", "tensor"),
            P(None, "tensor"),
            P(None, "tensor"),
        ),
        check_vma=False,
    )
```

```python
import functools

import jax
import jax.numpy as jnp
from jax import lax
from jax.experimental import pallas as pl
from jax.experimental.pallas import tpu as pltpu
from jax.sharding import PartitionSpec as P

HEAD_DIM = 64
EPSILON = 1e-05
LANES = 128
VLIM = 32
BETWEEN = 4
WAITED = 3
LATE = 4
PLIM = 24
GROUP = 8
KIND_IN, KIND_OUT = 1, 3
EXTRA = 8
ROWS = 128

F32 = jnp.float32
BF16 = jnp.bfloat16
EXACT = lax.Precision.HIGHEST


def iota(shape, dim):
    return lax.broadcasted_iota(jnp.int32, shape, dim)


def mm(a, b, da=1, db=0, precision=None):
    return lax.dot_general(
        a, b, (((da,), (db,)), ((), ())), precision=precision, preferred_element_type=F32
    )


def two_heads(table, first):
    rows = table.shape[0]
    left = jnp.broadcast_to(table[:, first : first + 1], (rows, LANES))
    right = jnp.broadcast_to(table[:, first + 1 : first + 2], (rows, LANES))
    return jnp.where(iota((rows, LANES), 1) < HEAD_DIM, left, right)


def spread_weights(wide, kind, width):
    lane, col = iota((LANES, width), 0), iota((LANES, width), 1)
    part = lane // GROUP
    hit = ((part == kind) | (part == kind + 1)) & ((lane & (GROUP - 1)) == col // HEAD_DIM)
    return mm(wide, jnp.where(hit, 1.0, 0.0).astype(BF16))


def split_queries(queries, doc_start):
    rows, width = queries.shape
    ahead = iota((rows, width), 0) < doc_start
    wide = queries.astype(F32)
    both = [jnp.where(ahead, wide, 0.0), jnp.where(ahead, 0.0, wide)]
    return jnp.concatenate(both, axis=1).astype(BF16)


def tile(p):
    return slice(p * LANES, (p + 1) * LANES)


def row_block(i):
    return slice(i * ROWS, (i + 1) * ROWS)


def each_pair(one):
    def step(p, carry):
        one(p, pl.ds(pl.multiple_of(p * LANES, LANES), LANES))
        return carry

    lax.fori_loop(0, GROUP // 2, step, 0)


def each_block(rows, one):
    def step(i, carry):
        one(pl.ds(pl.multiple_of(i * ROWS, ROWS), ROWS))
        return carry

    lax.fori_loop(0, rows // ROWS, step, 0)


def turn(table, p):
    return pltpu.roll(table, lax.rem(LANES - 2 * p, LANES), 1)


def call(kernel, outs, ins, out_shapes, scratch=(), alias=None, limit=16, steps=1):
    return pl.pallas_call(
        kernel,
        grid=(steps,),
        in_specs=ins,
        out_specs=outs,
        out_shape=out_shapes,
        scratch_shapes=list(scratch),
        input_output_aliases=alias or {},
        cost_estimate=pl.CostEstimate(flops=0, bytes_accessed=0, transcendentals=0),
        compiler_params=pltpu.CompilerParams(vmem_limit_bytes=limit * 2**20),
    )


def whole(array):
    zeros = (0,) * array.ndim
    return pl.BlockSpec(array.shape, lambda s: zeros)


def columns(array, k, width):
    lead = (0,) * (array.ndim - 1)
    return pl.BlockSpec(array.shape[:-1] + (width,), lambda s: lead + (k,))


SCALAR = pl.BlockSpec(memory_space=pltpu.SMEM)
ANYWHERE = pl.BlockSpec(memory_space=pl.ANY)


def silu(value):
    sigmoid = 0.5 + 0.5 * jnp.tanh(0.5 * value)
    return value * sigmoid, sigmoid


def open_kernel(
    k, doc, step_ref, keys, seq, prompt_in, prompt_keys, rate, state,
    tab_ref, wide_ref, first_ref, move_ref, late_ref, mine_ref, through_ref, low_ref, cols_ref,
):
    heads, rows = step_ref.shape[1:]
    doc_start = doc[0, 0]
    step = step_ref[0]
    hh, ll = iota((heads, LANES), 0), iota((heads, LANES), 1)
    spread = jnp.where((ll < 5 * GROUP) & (hh == k * GROUP + (ll & (GROUP - 1))), 1.0, 0.0)
    spread = spread.astype(BF16)
    tri = jnp.where(iota((rows, rows), 0) >= iota((rows, rows), 1), 1.0, 0.0).astype(BF16)
    high = step.astype(BF16)
    rest = step - high.astype(F32)
    middle = rest.astype(BF16)
    low = (rest - middle.astype(F32)).astype(BF16)
    step_rep = jnp.zeros((rows, LANES), F32)
    cum = jnp.zeros((rows, LANES), F32)
    for part in (low, middle, high):
        rep = mm(part, spread, 0, 0)
        step_rep = step_rep + rep
        cum = cum + mm(tri, rep.astype(BF16))
    before = cum - step_rep
    pos = iota((rows, LANES), 0)
    kind = iota((rows, LANES), 1) // GROUP
    has = doc_start < rows
    ex_start = jnp.sum(jnp.where(pos == doc_start, before, 0.0), axis=0, keepdims=True)
    end = cum[rows - 1 : rows]
    tail_start = jnp.where(has, doc_start, 0)
    arg = jnp.where(kind < KIND_OUT, jnp.where(pos < doc_start, 0.0, ex_start) - cum, cum - end)
    keep = (kind < KIND_OUT) | (pos >= tail_start)
    weights = jnp.where(keep, jnp.exp(jnp.minimum(arg, 0.0)), 0.0)
    tab_ref[...] = cum
    head_part = weights.astype(BF16).astype(F32)
    is_head = (kind == KIND_IN) | (kind == KIND_OUT)
    wide = jnp.where(is_head, head_part, weights - head_part).astype(BF16)
    wide_ref[...] = wide
    through = jnp.where(has, 0.0, jnp.exp(-end))
    leave = jnp.where(has, jnp.exp(ex_start - end), 0.0)

    prompt_rows = rate.shape[0]
    square = (prompt_rows, prompt_rows)
    later = jnp.where(iota(square, 0) < iota(square, 1), 1.0, 0.0)
    spread_weight = jnp.exp(-mm(later, rate[...], precision=EXACT))
    carry = jnp.exp(-jnp.sum(rate[...], axis=0, keepdims=True))
    for p in range(GROUP // 2):
        cols_ref[:prompt_rows, tile(p)] = two_heads(spread_weight, k * GROUP + 2 * p)
        for place, row in ((0, two_heads(carry, k * GROUP + 2 * p)), (8, two_heads(through, 2 * p))):
            rows_here = slice(prompt_rows + place, prompt_rows + place + 8)
            cols_ref[rows_here, tile(p)] = jnp.broadcast_to(row, (8, LANES))
        cols_ref[prompt_rows + 16 : prompt_rows + 24, tile(p)] = jnp.broadcast_to(
            two_heads(leave, 2 * p), (8, LANES)
        )
    state_rows, width = state.shape
    weighted = (seq[0].astype(F32) * spread_weights(wide, KIND_OUT, width)).astype(BF16)
    field = mm(
        prompt_keys[...].astype(F32), cols_ref[:prompt_rows] * prompt_in[...].astype(F32), 0, 0, EXACT
    )
    start = field + cols_ref[prompt_rows : prompt_rows + 1] * state[...]
    through_cols = cols_ref[prompt_rows + 8 : prompt_rows + 9]
    through_ref[...] = jnp.broadcast_to(through_cols, through_ref.shape)
    leave_cols = cols_ref[prompt_rows + 16 : prompt_rows + 17]
    move = mm(keys[0], weighted, 0, 0) + leave_cols * start
    is_first = lax.axis_index("ctx") == 0
    low_ref[...] = start.astype(BF16)
    mine_ref[:state_rows] = jnp.where(is_first, start, 0.0)
    move_ref[:state_rows] = move
    late_ref[:state_rows] = move
    first_ref[:state_rows] = through_cols * start + move
    ones = jnp.ones((EXTRA, width), F32)
    mine_ref[state_rows:] = jnp.where(is_first, ones, 0.0)
    extra = jnp.broadcast_to(leave_cols, (EXTRA, width))
    move_ref[state_rows:] = extra
    late_ref[state_rows:] = extra
    first_ref[state_rows:] = through_cols + extra


def open_from_hbm(ks, cut, outs, doc, *refs):
    ins = len(cut)
    held, buffers, sems = refs[:ins], refs[-1 - ins : -1], refs[-1]
    made = refs[-1 - ins - outs * len(ks) : -1 - ins]
    copies = []
    for n, (source, buffer) in enumerate(zip(held, buffers)):
        width = buffer.shape[-1]
        columns_here = pl.ds(ks[0] * (width // len(ks)) if cut[n] else 0, width)
        lead = (slice(None),) * (len(buffer.shape) - 1)
        copies.append(pltpu.make_async_copy(source.at[lead + (columns_here,)], buffer, sems.at[n]))
    for copy in copies:
        copy.start()
    for copy in copies:
        copy.wait()
    for place, k in enumerate(ks):
        mine = []
        for buffer, is_cut in zip(buffers, cut):
            width = buffer.shape[-1] // len(ks)
            lead = (slice(None),) * (len(buffer.shape) - 1)
            mine.append(buffer.at[lead + (pl.ds(place * width, width),)] if is_cut else buffer)
        open_kernel(k, doc, *mine, *made[place * outs : (place + 1) * outs])


def step_kernel(arrived, move, through, *rest):
    mine, (sum_ref, send_ref) = rest[:-2], rest[-2:]
    total = arrived[...] if not mine else mine[0][...] + arrived[...]
    sum_ref[...] = total
    send_ref[...] = through[: total.shape[0]] * total + move[...]


def head_halves():
    lane = iota((1, LANES), 1)
    return [jnp.where(half, 1.0, 0.0).astype(BF16) for half in (lane < HEAD_DIM, lane >= HEAD_DIM)]


def within_kernel(k, doc, tab_ref, keys, queries, seq, skip, base_ref, cum_rows, scores, skips):
    rows = tab_ref.shape[0]
    doc_start = doc[0, 0]
    halves = head_halves()
    turned_sums = jnp.transpose(tab_ref[...])
    for h in range(GROUP):
        cum_rows[h] = jnp.broadcast_to(turned_sums[h : h + 1], cum_rows.shape[1:])
    for p in range(GROUP // 2):
        skips[:, tile(p)] = jnp.broadcast_to(two_heads(skip[...], k * GROUP + 2 * p), (8, LANES))
    for i in range(rows // ROWS):
        upto = (i + 1) * ROWS
        t = iota((ROWS, upto), 0) + i * ROWS
        s = iota((ROWS, upto), 1)
        same = (s <= t) & ((t < doc_start) | (s >= doc_start))
        scores[row_block(i), :upto] = jnp.where(same, mm(queries[0, row_block(i)], keys[0, :upto], 1, 1), 0.0)

    def pair(p, here):
        turned = turn(tab_ref[...], p)
        values = [seq[0, :, here] * half for half in halves]
        for i in range(rows // ROWS):
            upto = (i + 1) * ROWS
            total = skips[:1, here] * seq[0, row_block(i), here].astype(F32)
            for half in range(2):
                gap = cum_rows[2 * p + half, :1, :upto] - turned[row_block(i), half : half + 1]
                mixing = (scores[row_block(i), :upto] * jnp.exp(jnp.minimum(gap, 0.0))).astype(BF16)
                total += mm(mixing, values[half][:upto])
            base_ref[row_block(i), here] = total

    each_pair(pair)


def gate_kernel(
    doc, wide, base, mine, arrived, low, queries, gate, grad, gain, before, *rest
):
    out_ref, stat_ref, share_ref = rest[-3:]
    rows, width = base.shape
    state_rows = low.shape[0]
    state_in = mine[...] + arrived[...]
    share_ref[...] = state_in[state_rows:]
    fields = jnp.concatenate([state_in[:state_rows].astype(BF16), low[...]], axis=0)
    reads = mm(split_queries(queries[0], doc[0, 0]), fields)
    weights = spread_weights(wide[...], KIND_IN, width)
    for i in range(rows // ROWS):
        rb = row_block(i)
        squares = jnp.zeros((ROWS, LANES), F32)
        inner = jnp.zeros((ROWS, LANES), F32)
        for p in range(GROUP // 2):
            out = (base[rb, tile(p)] + weights[rb, tile(p)] * reads[rb, tile(p)]).astype(BF16)
            out_ref[rb, tile(p)] = out
            act, _ = silu(gate[0, rb, tile(p)].astype(F32))
            gated = out.astype(F32) * act
            squares += gated * gated
            inner += grad[0, rb, tile(p)].astype(F32) * gain[:, tile(p)] * gated
        lane = iota((ROWS, 8), 1)
        sums = jnp.where(
            lane == 0,
            jnp.sum(squares, axis=1, keepdims=True),
            jnp.where(lane == 1, jnp.sum(inner, axis=1, keepdims=True), 0.0),
        )
        stat_ref[rb] = sums if before is None else before[rb] + sums


def norm_factors(inner_cols, stat):
    inverse = lax.rsqrt(stat[:, 0:1] / inner_cols + EPSILON)
    pull = stat[:, 1:2] * inverse * inverse * inverse / inner_cols
    shape = (stat.shape[0], LANES)
    return jnp.broadcast_to(inverse, shape), jnp.broadcast_to(pull, shape)


def visit_kernel(
    inner_cols, chunks, doc, stat_a, stat_b, out, gate, grad, gain, queries, share, *rest
):
    wides, ssd_ref, weighted, part = rest[:chunks], rest[chunks], rest[-2], rest[-1]
    visits, parts = rest[chunks + 1 : 2 * chunks + 1], rest[2 * chunks + 1 : -2]
    wide = wides[0][...]
    for n in range(1, chunks):
        wide = jnp.where(pl.program_id(0) == n, wides[n][...], wide)
    rows, width = out.shape
    state_rows = queries.shape[2]
    weights = spread_weights(wide, KIND_IN, width)
    for i in range(rows // ROWS):
        rb = row_block(i)
        inverse, pull = norm_factors(inner_cols, stat_a[rb] + stat_b[rb])
        for p in range(GROUP // 2):
            act, _ = silu(gate[0, rb, tile(p)].astype(F32))
            gated = out[rb, tile(p)].astype(F32) * act
            scaled = grad[0, rb, tile(p)].astype(F32) * gain[:, tile(p)]
            ssd = ((inverse * scaled - gated * pull) * act).astype(BF16)
            ssd_ref[rb, tile(p)] = ssd
            weighted[rb, tile(p)] = (weights[rb, tile(p)] * ssd.astype(F32)).astype(BF16)
    both = mm(split_queries(queries[0], doc[0, 0]), weighted[...], 0, 0)
    visit = both[:state_rows]
    for n, visit_ref in enumerate(visits):

        @pl.when(pl.program_id(0) == n)
        def _(visit_ref=visit_ref):
            visit_ref[...] = visit

    part[...] = both[state_rows:] + share[:1] * visit
    span = state_rows // len(parts)
    for d, piece in enumerate(parts):
        owner = lax.rem(lax.axis_index("dp") + d, len(parts))
        piece[...] = part[pl.ds(pl.multiple_of(owner * span, span), span)]


def back_kernel(
    k, inner_cols, doc, tab_ref, keys, queries, stat_a, stat_b, out, gate, grad, gain, ssd_grad, skip, *rest
):
    base_ref, normed_ref, gate_grad_ref, cum_rows, scores, skips = rest[-6:]
    rows = tab_ref.shape[0]
    doc_start = doc[0, 0]
    halves = head_halves()
    turned_sums = jnp.transpose(tab_ref[...])
    for h in range(GROUP):
        cum_rows[h] = jnp.broadcast_to(turned_sums[h : h + 1], cum_rows.shape[1:])
    for p in range(GROUP // 2):
        skips[:, tile(p)] = jnp.broadcast_to(two_heads(skip[...], k * GROUP + 2 * p), (8, LANES))
    for i in range(rows // ROWS):
        down = i * ROWS
        s = iota((ROWS, rows - down), 0) + down
        t = iota((ROWS, rows - down), 1) + down
        same = (s <= t) & ((t < doc_start) | (s >= doc_start))
        scores[row_block(i), down:] = jnp.where(same, mm(keys[0, row_block(i)], queries[0, down:], 1, 1), 0.0)

    def pair(p, here):
        turned = turn(tab_ref[...], p)
        grads = [ssd_grad[:, here] * half for half in halves]
        for i in range(rows // ROWS):
            down = i * ROWS
            total = skips[:1, here] * ssd_grad[row_block(i), here].astype(F32)
            for half in range(2):
                gap = turned[row_block(i), half : half + 1] - cum_rows[2 * p + half, :1, down:]
                mixing = (scores[row_block(i), down:] * jnp.exp(jnp.minimum(gap, 0.0))).astype(BF16)
                total += mm(mixing, grads[half][down:])
            base_ref[row_block(i), here] = total

    each_pair(pair)

    def one(rb):
        inverse, pull = norm_factors(inner_cols, stat_a[rb] + stat_b[rb])
        for p in range(GROUP // 2):
            value = gate[0, rb, tile(p)].astype(F32)
            act, sigmoid = silu(value)
            slope = sigmoid * (1.0 + value * (1.0 - sigmoid))
            wide_out = out[rb, tile(p)].astype(F32)
            gated = wide_out * act
            gains = gain[:, tile(p)]
            scaled = grad[0, rb, tile(p)].astype(F32) * gains
            normed_ref[0, rb, tile(p)] = (gated * inverse * gains).astype(BF16)
            gated_grad = inverse * scaled - gated * pull
            gate_grad_ref[0, rb, tile(p)] = (gated_grad * wide_out * slope).astype(BF16)

    each_block(rows, one)


def close_kernel(wide, base, adjoint, arrived, keys, *rest):
    grad_ref = rest[-1]
    total = arrived[...] if adjoint is None else adjoint[...] + arrived[...]
    reads = mm(keys[0], total.astype(BF16))
    weights = spread_weights(wide[...], KIND_OUT, base.shape[1])
    grad_ref[0] = (base[...] + weights * reads).astype(BF16)


def add_kernel(*refs):
    refs[-1][...] = sum((r[...] for r in refs[1:-1]), refs[0][...])


def split_add_kernel(parts, *refs):
    total, pieces = refs[-1], refs[-1 - parts : -1]
    span = total.shape[1]
    for n in range(parts):
        rows = slice(n * span, (n + 1) * span)
        total[n] = sum((r[rows] for r in refs[1 : -1 - parts]), refs[0][rows])
    for d, piece in enumerate(pieces):
        piece[...] = total[lax.rem(lax.axis_index("ctx") + d, parts)]


def join_kernel(parts, *refs):
    out, total = refs[-2:]
    span = total.shape[1]
    for d, piece in enumerate(refs[:parts]):
        total[lax.rem(lax.axis_index("ctx") + parts - d, parts)] = piece[...]
    for n in range(parts):
        out[n * span : (n + 1) * span] = total[n]


def derive_kernel(chunks, pieces, prompt_keys, *rest):
    cols, parts = rest[:chunks], rest[chunks : chunks + pieces]
    prompt_ref, start_ref, total = rest[chunks + pieces :]
    span = parts[0].shape[0]
    for d, piece in enumerate(parts):
        owner = lax.rem(lax.axis_index("dp") + pieces - d, pieces)
        total[pl.ds(pl.multiple_of(owner * span, span), span)] = piece[...]
    prompt_rows = prompt_keys.shape[0]
    keys = prompt_keys[...].astype(F32)
    for k in range(chunks):
        width = cols[k].shape[1]
        span = slice(k * width, (k + 1) * width)
        grads = total[:, span]
        start_ref[:, span] = cols[k][prompt_rows : prompt_rows + 1] * grads
        prompt_ref[:, span] = cols[k][:prompt_rows] * mm(keys, grads, precision=EXACT)


def ring(count, distance):
    return [(i, (i + distance) % count) for i in range(count)]


def shape(*dims, dtype=F32):
    return jax.ShapeDtypeStruct(dims, dtype)


def body(
    seq_in,
    gate_in,
    keys_in,
    queries_in,
    step_rate,
    doc_starts,
    skip_gain,
    norm_gain,
    prompt_in,
    prompt_keys,
    prompt_rate,
    start_state,
    out_grad,
):
    _, rows, cols = seq_in.shape
    state_rows = keys_in.shape[2]
    heads = step_rate.shape[2]
    prompt_rows = prompt_in.shape[0]
    chunks = heads // GROUP
    width = cols // chunks
    tensors = lax.axis_size("tensor")
    inner_cols = cols * tensors
    count = lax.axis_size("ctx")
    step = jnp.swapaxes(step_rate, 1, 2)
    skip = skip_gain.reshape(1, heads)
    gain = norm_gain.reshape(1, cols)
    each = range(chunks)
    message = shape(state_rows + EXTRA, width)
    summary = shape(state_rows, width)
    block = shape(rows, width)
    block_low = shape(rows, width, dtype=BF16)
    full = shape(*seq_in.shape, dtype=BF16)
    part_shape = shape(state_rows, cols)

    def blocked(array, k):
        return columns(array, k, width)

    def run(kernel, out, ins, after=(), hold=(), alias=None, scratch=(), limit=16, steps=1):
        held = len(ins) + len(after)
        made = held + len(hold)

        def ordered(*refs):
            kernel(*refs[: len(ins)], *refs[made : made + len(out)], *refs[made + len(out) + len(hold) :])

        extra = [(a, ANYWHERE) for a in (*after, *hold)]
        out = list(out)
        results = out + [(shape(*h.shape, dtype=h.dtype), ANYWHERE) for h in hold]
        return call(
            ordered,
            [whole(s) if spec is None else spec for s, spec in results],
            [whole(a) if spec is None else spec for a, spec in ins + extra],
            [s for s, _ in results],
            alias={**(alias or {}), **{held + i: len(out) + i for i in range(len(hold))}},
            scratch=scratch,
            limit=limit,
            steps=steps,
        )(*[a for a, _ in ins + extra])

    tabs, wides, firsts, moves, lates, sums, throughs, lows, col_tabs = ([] for _ in range(9))
    made = (tabs, wides, firsts, moves, lates, sums, throughs, lows, col_tabs)
    made_shapes = [
        shape(rows, LANES),
        shape(rows, LANES, dtype=BF16),
        message,
        message,
        message,
        message,
        message,
        shape(state_rows, width, dtype=BF16),
        shape(prompt_rows + 24, width),
    ]

    def open_chunks(ks, after):
        ins = [
            (step, False),
            (keys_in, False),
            (seq_in, True),
            (prompt_in, True),
            (prompt_keys, False),
            (prompt_rate, False),
            (start_state, True),
        ]
        cut = [c for _, c in ins]
        blocks = [a.shape[:-1] + (len(ks) * width,) if c else a.shape for a, c in ins]
        out = run(
            functools.partial(open_from_hbm, ks, cut, len(made)),
            [(s, None) for s in made_shapes] * len(ks),
            [(doc_starts, SCALAR)] + [(a, ANYWHERE) for a, _ in ins],
            after=after,
            scratch=[pltpu.VMEM(b, a.dtype) for b, (a, _) in zip(blocks, ins)]
            + [pltpu.SemaphoreType.DMA((len(ins),))],
            limit=60 if ks[0] == 0 else PLIM,
        )
        for place, k in enumerate(ks):
            for held, one in zip(made, out[place * len(made) :]):
                held.append(one)
            arrived[k] = edge_up(firsts[k], 0)

    def chain_step(k, arrived, move, mine, after=()):
        return run(
            step_kernel,
            [(shape(*move.shape), None)] * 2,
            [(arrived, None), (move, None), (throughs[k], None)] + [(m, None) for m in mine],
            after=after,
        )

    def edge_up(array, edge):
        return lax.ppermute(array, "ctx", [(edge, edge + 1)])

    mixing_scratch = [pltpu.VMEM(s, F32) for s in ((GROUP, 8, rows), (rows, rows), (8, width))]

    def within(k, after, hold):
        base, *held = run(
            functools.partial(within_kernel, k),
            [(block, None)],
            [
                (doc_starts, SCALAR),
                (tabs[k], None),
                (keys_in, None),
                (queries_in, None),
                (seq_in, blocked(seq_in, k)),
                (skip, None),
            ],
            after=after,
            hold=hold,
            scratch=mixing_scratch,
        )
        bases.append(base)
        return held

    outs, shares, stats, bases = [], [], [], []
    out_shape, share_shape = shape(rows, cols, dtype=BF16), shape(EXTRA, cols)


    def gates(k, hold):
        kernel, held, alias = gate_kernel, [], {}
        if stats:
            held = [(stats[-1], None), (outs[-1], ANYWHERE), (shares[-1], ANYWHERE)]
            alias = {11: 0, 12: 2}
        else:
            kernel = lambda *refs: gate_kernel(*refs[:10], None, *refs[10:])
        out, stat, share, *held = run(
            kernel,
            [
                (out_shape, blocked(out_shape, k)),
                (shape(rows, 8), None),
                (share_shape, blocked(share_shape, k)),
            ],
            [
                (doc_starts, SCALAR),
                (wides[k], None),
                (bases[k], None),
                (sums[k], None),
                (arrived[k], None),
                (lows[k], None),
                (queries_in, None),
                (gate_in, blocked(gate_in, k)),
                (out_grad, blocked(out_grad, k)),
                (gain, blocked(gain, k)),
            ]
            + held,
            alias=alias,
            hold=hold,
        )
        outs.append(out)
        shares.append(share)
        stats.append(stat)
        return held

    last = count - 2
    arrived = [None] * chunks
    open_chunks([0], [])
    pairs = [list(each)[k : k + 2] for k in range(1, chunks, 2)]
    for ks in pairs[:1]:
        open_chunks(ks, [])
    for edge in range(1, max(last, 2)):
        for k in each:
            sent = []
            if edge < last:
                sums[k], *sent = chain_step(k, arrived[k], moves[k], [sums[k]])
                arrived[k] = edge_up(sent[0], edge)
            if edge == 1 and k + 1 < len(pairs):
                open_chunks(pairs[k + 1], sent)
    lag = 2
    for k in range(chunks + lag):
        if k < chunks:
            if k >= lag:
                gates(k - lag, [])
            sent = []
            if last > 0:
                sums[k], *sent = chain_step(k, arrived[k], lates[k], [sums[k]])
                arrived[k] = edge_up(sent[0], last)
            lates[k + 1 : k + 2] = within(k, sent, lates[k + 1 : k + 2])
        else:
            gates(k - lag, [])
    stat = stats[-1]
    other = lax.ppermute(stat, "tensor", ring(tensors, 1))

    def edge_down(array, edge):
        return lax.ppermute(array, "ctx", [(edge, edge - 1)])

    def edge_down(array, edge):
        return lax.ppermute(array, "ctx", [(edge, edge - 1)])

    def moving(array, width):
        lead = (0,) * (array.ndim - 1)
        return pl.BlockSpec(array.shape[:-1] + (width,), lambda s: lead + (s,))

    groups = lax.axis_size("dp")
    piece = shape(state_rows // groups, cols)
    result = run(
        functools.partial(visit_kernel, inner_cols, chunks),
        [(out_shape, moving(out_shape, width))] + [(summary, None)] * chunks + [(piece, moving(piece, width))] * groups,
        [
            (doc_starts, SCALAR),
            (stat, None),
            (other, None),
            (outs[-1], moving(outs[-1], width)),
            (gate_in, moving(gate_in, width)),
            (out_grad, moving(out_grad, width)),
            (gain, moving(gain, width)),
            (queries_in, None),
            (shares[-1], moving(shares[-1], width)),
        ]
        + [(w, None) for w in wides],
        scratch=[pltpu.VMEM((rows, width), BF16), pltpu.VMEM((state_rows, width), F32)],
        steps=chunks,
        limit=VLIM,
    )
    ssd_grad, visits, parts = result[0], result[1 : 1 + chunks], result[1 + chunks :]
    for k in each:
        arrived[k] = edge_down(visits[k], count - 1)

    back_bases = []
    normed = gate_grad = None

    def back(k, after, hold):
        ins = [
            (doc_starts, SCALAR),
            (tabs[k], None),
            (keys_in, None),
            (queries_in, None),
            (stat, None),
            (other, None),
            (outs[-1], blocked(outs[-1], k)),
            (gate_in, blocked(gate_in, k)),
            (out_grad, blocked(out_grad, k)),
            (gain, blocked(gain, k)),
            (ssd_grad, blocked(ssd_grad, k)),
            (skip, None),
        ]
        alias = {}
        if normed is not None:
            alias = {len(ins): 1, len(ins) + 1: 2}
            ins += [(normed, ANYWHERE), (gate_grad, ANYWHERE)]
        base, *results = run(
            functools.partial(back_kernel, k, inner_cols),
            [(block, None), (full, blocked(full, k)), (full, blocked(full, k))],
            ins,
            after=after,
            hold=hold,
            alias=alias,
            scratch=mixing_scratch,
        )
        back_bases.append(base)
        return results

    normed, gate_grad, *parts = back(0, [], list(parts))
    from_groups = [lax.ppermute(parts[d], "dp", ring(groups, d)) for d in range(1, groups)]
    adjoints = [None] * chunks
    sent = []
    for edge in range(count - 2, 0, -1):
        for k in each:
            held = [] if adjoints[k] is None else [adjoints[k]]
            order = back_bases[-1:] if edge == 1 else []
            adjoints[k], message_out = chain_step(k, arrived[k], visits[k], held, order)
            sent = [message_out]
            arrived[k] = edge_down(message_out, edge)
            if edge == 1 and 0 < k < BETWEEN:
                normed, gate_grad = back(k, sent + [arrived[k - 1]], [])

    small = shape(piece.shape[0] // count, cols)
    mine = run(
        functools.partial(split_add_kernel, count),
        [(small, None)] * count,
        [(p, None) for p in (parts[0], *from_groups)],
        after=sent + back_bases[-1:] + arrived[WAITED : WAITED + 1],
        scratch=[pltpu.VMEM((count,) + small.shape, F32)],
    )
    from_blocks = [lax.ppermute(mine[d], "ctx", ring(count, d)) for d in range(1, count)]
    for k in range(len(back_bases), LATE):
        normed, gate_grad = back(k, [mine[0], arrived[k]], [])
    (own,) = run(add_kernel, [(small, None)], [(p, None) for p in (mine[0], *from_blocks)], after=back_bases[-1:])
    owned = [own] + [lax.ppermute(own, "ctx", ring(count, d)) for d in range(1, count)]
    for k in range(LATE, chunks):
        normed, gate_grad = back(k, [own, arrived[k]], [])
    (total,) = run(
        functools.partial(join_kernel, count),
        [(piece, None)],
        [(p, None) for p in owned],
        after=back_bases[-1:],
        scratch=[pltpu.VMEM((count,) + small.shape, F32)],
    )
    totals = [total] + [lax.ppermute(total, "dp", ring(groups, d)) for d in range(1, groups)]

    grad_in = None
    for k in each:
        ins = [(wides[k], None), (back_bases[k], None)]
        kernel = close_kernel
        if adjoints[k] is None:
            kernel = lambda wide, base, *refs: close_kernel(wide, base, None, *refs)
        else:
            ins.append((adjoints[k], None))
        ins += [(arrived[k], None), (keys_in, None)]
        alias = {}
        if grad_in is not None:
            alias = {len(ins): 0}
            ins.append((grad_in, ANYWHERE))
        (grad_in,) = run(kernel, [(full, blocked(full, k))], ins, alias=alias)

    grad_prompt, grad_start = run(
        functools.partial(derive_kernel, chunks, groups),
        [(shape(prompt_rows, cols), None), (part_shape, None)],
        [(a, None) for a in (prompt_keys, *col_tabs, *totals)],
        scratch=[pltpu.VMEM((state_rows, cols), F32)],
    )
    return normed, grad_in, gate_grad, grad_prompt, grad_start


def solution(mesh):
    return jax.shard_map(
        body,
        mesh=mesh,
        in_specs=(
            P("dp", "ctx", "tensor"),
            P("dp", "ctx", "tensor"),
            P("dp", "ctx", None),
            P("dp", "ctx", None),
            P("dp", "ctx", "tensor"),
            P("dp", "ctx"),
            P("tensor"),
            P("tensor"),
            P(None, "tensor"),
            P(),
            P(None, "tensor"),
            P(None, "tensor"),
            P("dp", "ctx", "tensor"),
        ),
        out_specs=(
            P("dp", "ctx", "tensor"),
            P("dp", "ctx", "tensor"),
            P("dp", "ctx", "tensor"),
            P(None, "tensor"),
            P(None, "tensor"),
        ),
        check_vma=False,
    )
```
